32 devices in a mesh: groups: 2 (over y), dp: 16 (over z, x, core).
Axes of the slice: x: 2, y: 2, z: 4, core: 2. Of those that a mesh axis runs over, the one named last changes fastest.
Arguments:
- tokens: bfloat16 [256, 8192], P(('groups', 'dp')), parts along dimension 0, may hold values from -6 to 6
- token_adapter_index: int32 [256, 1], P(('groups', 'dp')), parts along dimension 0, may hold values from 0 to 15; in each aligned block of 128 rows (0 to 127, 128 to 255, ...) at most 32 rows name the same one
- adapter_slot_index: int32 [16], replicated, may hold values from 0 to 15, each once
- gate_matrix: bfloat16 [8192, 28672], P(None, 'dp'), may hold values from -0.0625 to 0.0625
- up_matrix: bfloat16 [8192, 28672], P(None, 'dp'), may hold values from -0.0625 to 0.0625
- adapter_down_factor: bfloat16 [16, 8192, 64], P('dp'), may hold values from -0.0625 to 0.0625
- adapter_up_factor: bfloat16 [16, 64, 28672], P('dp'), may hold values from -0.75 to 0.75
Outputs:
- hidden: bfloat16 [256, 28672], P('groups', 'dp'), parts along dimension 0
The draws below stay inside these ranges and needn't reach their ends.
There are 2 independent parts, one for each index of `groups`. The reference program is written for one: setup_inputs(seed, part) draws one part's arguments, and reference() takes and returns one part's arrays. A program takes and returns all parts, laid end to end along the dimension named above; an argument that names none is the same for every part. Nothing has to cross between parts.
Inputs may be any that keep to these rules, and one draw needn't show every extreme that they name: `token_adapter_index`: no adapter is named by more than 32 rows of a group, and one is named by exactly 32. `adapter_slot_index`: each slot holds exactly one adapter.
All inputs are finite; a program needn't handle non-finite values.
Results may differ from the reference program's by a relative error of at most 0.0075.
Values may be sent and summed in bfloat16 or wider, within the bound.
No kernel may reach another device: no remote copies, remote signals or barrier semaphores. Data moves between devices by JAX's collectives and lax.ppermute only.
A program may use at most 192 MiB of HBM per device.

```python
import math
import jax
import jax.numpy as jnp
import numpy as np
from jax import lax

MODEL_WIDTH = 8192
HIDDEN_WIDTH = 28672
ADAPTER_RANK = 64
CAP = 32
TOKENS = 128
ADAPTER_SLOTS = 16


def shard_levels(stream_key, shape, split, low, largest):
    def one(dim, parts):
        heights = jax.random.uniform(jax.random.fold_in(jax.random.fold_in(stream_key, 6), dim), (parts,), jnp.float32, low / len(split), largest / len(split))
        return jnp.repeat(jnp.exp(heights), shape[dim] // parts).reshape((-1,) + (1,) * (len(shape) - dim - 1))

    level = one(*split[0])
    for cut in split[1:]:
        level = level * one(*cut)
    return level


def assign_block(key, own, number, rows, amount, top, most, lean):
    sequence = jax.random.permutation(key, amount)
    crowded, usual = load_shares(amount, rows * top, most, lean, True), load_shares(amount, rows * top, most, lean, False)
    places = jnp.arange(amount)

    def named(sizes, offset_by):
        used = int((sizes > 0).sum())
        fixed = max(1, used // 4)
        moved = fixed + (places - fixed + offset_by * (used - fixed)) % max(1, amount - fixed)
        return jnp.zeros((amount,), jnp.int32).at[sequence[jnp.where(places < fixed, places, moved)]].set(jnp.asarray(sizes, jnp.int32))

    sizes = jnp.where(number % 4 == 0, named(crowded, number // 4), named(usual, number - number // 4 - 1))
    mixed = jax.random.permutation(jax.random.fold_in(own, 3), amount)
    donor, receiver = mixed[0:amount // 2 * 2:2], mixed[1:amount // 2 * 2:2]
    room = jnp.minimum(sizes[donor] - 1, most - sizes[receiver]) // 2
    room = jnp.where((donor == sequence[0]) | (receiver == sequence[0]) | (sizes[receiver] == 0), 0, jnp.maximum(room, 0))
    moved = jax.random.randint(jax.random.fold_in(own, 4), (amount // 2,), 0, 1 << 20) % (room + 1)
    sizes = sizes.at[donor].add(-moved).at[receiver].add(moved)
    labels = jnp.searchsorted(jnp.cumsum(sizes), jnp.arange(rows * top), side="right").astype(jnp.int32)
    table = labels.reshape(top, rows).T
    table = table[jax.random.permutation(jax.random.fold_in(own, 1), rows)]
    offset_by = jax.random.randint(jax.random.fold_in(own, 2), (rows, 1), 0, top)
    return jnp.take_along_axis(table, (jnp.arange(top)[None, :] + offset_by) % top, axis=1)


def load_shares(number_of, total, most, lean, full):
    weights = [(1 << 20) // math.isqrt(rank ** lean) + 1 for rank in range(1, number_of + 1)]
    largest = most if full else min(most, max(-(-total // number_of), total * weights[0] // sum(weights)))
    least = 1 if total - largest >= number_of - 1 else 0
    given, surplus = [largest] + [least] * (number_of - 1), total - largest - least * (number_of - 1)
    while surplus > 0:
        free = [i for i in range(1, number_of) if given[i] < largest] or [i for i in range(1, number_of) if given[i] < most]
        mass, left = sum([weights[i] for i in free]), surplus
        for i in free:
            more = min(most - given[i], max(1, left * weights[i] // mass), surplus)
            given[i] = given[i] + more
            surplus = surplus - more
    return np.array(given)


def gaussian(key, dims, width, bound, shards=(), held_as=jnp.bfloat16):
    gain = shard_levels(key, dims, shards, -0.22, 0.18) if shards else 1.0
    result = jax.random.normal(key, dims, jnp.float32) * width * gain
    return jnp.minimum(jnp.maximum(result, -bound), bound).astype(held_as)


def setup_inputs(seed: int = 0, part: int = 0) -> dict:
    arg_keys = jax.random.split(jax.random.key(seed), 8)
    own_keys = jax.random.split(jax.random.fold_in(arg_keys[7], part), 8)
    tokens = gaussian(own_keys[0], (TOKENS, MODEL_WIDTH), 1.0, 6.0, ((0, 16),))
    token_adapter_index_keys = jax.random.split(jax.random.fold_in(own_keys[1], 1), TOKENS // TOKENS)
    token_adapter_index_turns = jax.random.permutation(jax.random.fold_in(own_keys[1], 3), TOKENS // TOKENS)
    token_adapter_index = jax.vmap(lambda own, number: assign_block(jax.random.fold_in(own_keys[1], 2), own, number, TOKENS, ADAPTER_SLOTS, 1, CAP, 2))(token_adapter_index_keys, token_adapter_index_turns).reshape((TOKENS, 1))
    adapter_slot_index = jax.random.permutation(arg_keys[2], ADAPTER_SLOTS).astype(jnp.int32)
    gate_matrix = gaussian(arg_keys[3], (MODEL_WIDTH, HIDDEN_WIDTH), MODEL_WIDTH ** -0.5, 0.0625, ((1, 16),))
    up_matrix = gaussian(arg_keys[4], (MODEL_WIDTH, HIDDEN_WIDTH), MODEL_WIDTH ** -0.5, 0.0625, ((1, 16),))
    adapter_down_factor = gaussian(arg_keys[5], (ADAPTER_SLOTS, MODEL_WIDTH, ADAPTER_RANK), MODEL_WIDTH ** -0.5, 0.0625, ((0, 16),))
    adapter_up_factor = gaussian(arg_keys[6], (ADAPTER_SLOTS, ADAPTER_RANK, HIDDEN_WIDTH), ADAPTER_RANK ** -0.5, 0.75, ((0, 16),))
    return {"tokens": tokens, "token_adapter_index": token_adapter_index, "adapter_slot_index": adapter_slot_index, "gate_matrix": gate_matrix, "up_matrix": up_matrix, "adapter_down_factor": adapter_down_factor, "adapter_up_factor": adapter_up_factor}


def reference(tokens, token_adapter_index, adapter_slot_index, gate_matrix, up_matrix, adapter_down_factor, adapter_up_factor):
    ids = token_adapter_index[:, 0]
    slots = adapter_slot_index[ids].astype(jnp.int32)
    onehot = (slots[:, None] == jnp.arange(ADAPTER_SLOTS, dtype=jnp.int32)[None, :]).astype(jnp.int32)
    ranks = (jnp.sum(jnp.cumsum(onehot, 0) * onehot, 1) - 1).astype(jnp.int32)
    lookup_matrix = jnp.zeros((ADAPTER_SLOTS, CAP), jnp.int32).at[slots, ranks].set(jnp.arange(TOKENS, dtype=jnp.int32))

    def rows_by_slot(packed):
        rows, down, upper = packed
        selected_slot = tokens[rows]
        reduced_rows = jnp.dot(selected_slot, down, preferred_element_type=jnp.float32).astype(jnp.bfloat16)
        return jnp.dot(reduced_rows, upper, preferred_element_type=jnp.float32).astype(jnp.bfloat16)

    slot_block_list = lax.map(rows_by_slot, (lookup_matrix, adapter_down_factor, adapter_up_factor))
    delta = slot_block_list.reshape(ADAPTER_SLOTS * CAP, HIDDEN_WIDTH)[slots * CAP + ranks]
    gate = jnp.dot(tokens, gate_matrix, preferred_element_type=jnp.float32) + delta.astype(jnp.float32)
    up = jnp.dot(tokens, up_matrix, preferred_element_type=jnp.float32)
    return (jax.nn.silu(gate) * up).astype(jnp.bfloat16)
```

```python
import functools

import jax
import jax.numpy as jnp
from jax import lax
from jax.experimental import pallas as pl
from jax.experimental.pallas import tpu as pltpu
from jax.sharding import PartitionSpec as P

CAP = 32
LANES = 128
PLANES = 4
F32 = jnp.float32
BF16 = jnp.bfloat16


def general_shards(
    tokens,
    token_adapter_index,
    adapter_slot_index,
    gate_matrix,
    up_matrix,
    adapter_down_factor,
    adapter_up_factor,
):
    count = lax.axis_size("dp")
    myself = lax.axis_index("dp")
    all_rows, all_ids = (
        lax.all_gather(tokens, "dp", axis=0, tiled=True),
        lax.all_gather(token_adapter_index, "dp", axis=0, tiled=True),
    )
    total = all_rows.shape[0]
    places = jnp.arange(count, dtype=jnp.int32)
    match = all_ids[:, 0][:, None] == places[None, :]
    slots = jnp.sum(jnp.where(match, adapter_slot_index[None, :], 0), 1)
    slot_match = slots[:, None] == places[None, :]
    onehot = slot_match.astype(jnp.int32)
    ranks = jnp.sum(jnp.cumsum(onehot, 0) * onehot, 1) - 1
    capacity = CAP
    columns = jnp.arange(capacity, dtype=jnp.int32)
    mine = (slots == myself)[:, None] & (ranks[:, None] == columns[None, :])
    row_list = jnp.sum(jnp.where(mine, jnp.arange(total, dtype=jnp.int32)[:, None], 0), 0)
    selected_slot = jnp.take(all_rows, row_list, axis=0)
    reduced_rows = jnp.dot(
        selected_slot, adapter_down_factor[0], preferred_element_type=F32
    ).astype(BF16)
    slot_pieces = lax.all_to_all(adapter_up_factor, "dp", split_axis=2, concat_axis=0, tiled=True)
    all_low = lax.all_gather(reduced_rows, "dp", axis=0, tiled=True)
    rank_width = all_low.shape[1]
    token_low = jnp.take(all_low, slots * capacity + ranks, axis=0)
    expanded = (token_low[:, None, :] * slot_match.astype(BF16)[:, :, None]).reshape(
        total, count * rank_width
    )
    stacked = slot_pieces.reshape(count * rank_width, slot_pieces.shape[2])
    delta = jnp.dot(expanded, stacked, preferred_element_type=F32).astype(BF16)
    gate_base = jnp.dot(all_rows, gate_matrix, preferred_element_type=F32)
    up = jnp.dot(all_rows, up_matrix, preferred_element_type=F32)
    gate = gate_base + delta.astype(F32)
    return (jax.nn.silu(gate) * up).astype(BF16)


ANY = pl.BlockSpec(memory_space=pl.ANY)
CHUNKS = ((2, 3), (1, 0))


def repack_kernel(width, u_ref, *refs):
    outs, sems = refs[:-1], refs[-1]
    half = u_ref.shape[0] // 2
    me, y = lax.axis_index("dp"), lax.axis_index("groups")
    z, x, c = me // 4, (me // 2) % 2, me % 2
    copies = []
    for k, chunk in enumerate(CHUNKS):
        own, core, cross, both = outs[4 * k : 4 * k + 4]
        for i, j in enumerate(chunk):
            zz = lax.bitwise_xor(z, j)
            for ref, xx, cc, split in (
                (cross, 1 - x, c, True),
                (both, 1 - x, 1 - c, True),
                (core, x, 1 - c, False),
                (own, x, c, False),
            ):
                at = pl.multiple_of(((zz * 2 + xx) * 2 + cc) * width, LANES)
                rows = pl.ds(pl.multiple_of(y * half, half), half) if split else pl.ds(0, 2 * half)
                copies.append(
                    pltpu.make_async_copy(
                        u_ref.at[rows, pl.ds(at, width)],
                        ref.at[:, pl.ds(i * width, width)],
                        sems.at[len(copies)],
                    )
                )
    for copy in copies:
        copy.start()
    for copy in copies:
        copy.wait()


def repack(u, width):
    rank = u.shape[0]
    shapes = []
    for chunk in CHUNKS:
        n = len(chunk) * width
        shapes += [
            jax.ShapeDtypeStruct((rank, n), BF16),
            jax.ShapeDtypeStruct((rank, n), BF16),
            jax.ShapeDtypeStruct((rank // 2, n), BF16),
            jax.ShapeDtypeStruct((rank // 2, n), BF16),
        ]
    return pl.pallas_call(
        functools.partial(repack_kernel, width),
        out_shape=shapes,
        in_specs=[ANY],
        out_specs=[ANY] * len(shapes),
        scratch_shapes=[pltpu.SemaphoreType.DMA((16,))],
        cost_estimate=pl.CostEstimate(flops=0, bytes_accessed=3 * u.size, transcendentals=0),
        name="repack",
    )(u)


def delta_kernel(e_ref, *refs):
    stacked = jnp.concatenate([ref[...] for ref in refs[:-1]], axis=0)
    refs[-1][...] = jnp.dot(e_ref[...], stacked, preferred_element_type=F32).astype(BF16)


def delta_rows(e, parts, place, width):
    rows = e.shape[0]
    step = width // 2
    return pl.pallas_call(
        delta_kernel,
        out_shape=jax.ShapeDtypeStruct((rows, width), BF16),
        grid=(2,),
        in_specs=[pl.BlockSpec(e.shape, lambda i: (0, 0))]
        + [pl.BlockSpec((p.shape[0], step), lambda i: (0, 2 * place + i)) for p in parts],
        out_specs=pl.BlockSpec((rows, step), lambda i: (0, i)),
        cost_estimate=pl.CostEstimate(
            flops=2 * rows * e.shape[1] * width, bytes_accessed=2 * width * (rows + e.shape[1]), transcendentals=0
        ),
        name="delta_rows",
    )(e, *parts)


def base_kernel(xa_ref, xb_ref, g_ref, u_ref, gate_ref, up_ref):
    @pl.when(pl.program_id(0) == 0)
    def _():
        gate_ref[...] = jnp.zeros_like(gate_ref)
        up_ref[...] = jnp.zeros_like(up_ref)

    x = jnp.concatenate([xa_ref[...], xb_ref[...]], axis=0)
    gate_ref[...] += jnp.dot(x, g_ref[...], preferred_element_type=F32)
    up_ref[...] += jnp.dot(x, u_ref[...], preferred_element_type=F32)


def base(xa, xb, gate_matrix, up_matrix):
    depth, width = gate_matrix.shape
    block = 512
    rows = xa.shape[0]
    x_spec = pl.BlockSpec((rows, block), lambda k: (0, k))
    w_spec = pl.BlockSpec((block, width), lambda k: (k, 0))
    o_spec = pl.BlockSpec((2 * rows, width), lambda k: (0, 0))
    shape = jax.ShapeDtypeStruct((2 * rows, width), F32)
    return pl.pallas_call(
        base_kernel,
        out_shape=[shape, shape],
        grid=(depth // block,),
        in_specs=[x_spec, x_spec, w_spec, w_spec],
        out_specs=[o_spec, o_spec],
        compiler_params=pltpu.CompilerParams(vmem_limit_bytes=40 * 1024 * 1024),
        cost_estimate=pl.CostEstimate(
            flops=8 * rows * depth * width, bytes_accessed=4 * depth * width, transcendentals=0
        ),
        name="base",
    )(xa, xb, gate_matrix, up_matrix)


def finish_kernel(gate_ref, up_ref, pick_ref, order_ref, *refs):
    stacked = jnp.concatenate([ref[...] for ref in refs[:-1]], axis=0)
    delta = jnp.dot(pick_ref[...], stacked, preferred_element_type=F32)
    gate = gate_ref[...] + delta
    hidden = (gate / (1.0 + jnp.exp(-gate)) * up_ref[...]).astype(BF16)
    refs[-1][...] = jnp.dot(order_ref[...], hidden, preferred_element_type=F32).astype(BF16)


def finish(gate, up, pick, order, rows_by_plane):
    total, width = gate.shape
    step = width // 7 if width % (7 * LANES) == 0 else width
    col = lambda a: pl.BlockSpec((a.shape[0], step), lambda i: (0, i))
    whole = lambda a: pl.BlockSpec(a.shape, lambda i: (0, 0))
    return pl.pallas_call(
        finish_kernel,
        out_shape=jax.ShapeDtypeStruct((total, width), BF16),
        grid=(width // step,),
        in_specs=[col(gate), col(up), whole(pick), whole(order)] + [col(r) for r in rows_by_plane],
        out_specs=pl.BlockSpec((total, step), lambda i: (0, i)),
        cost_estimate=pl.CostEstimate(flops=0, bytes_accessed=4 * total * width * 4, transcendentals=total * width),
        name="finish",
    )(gate, up, pick, order, *rows_by_plane)


def plane_shards(
    tokens,
    token_adapter_index,
    adapter_slot_index,
    gate_matrix,
    up_matrix,
    adapter_down_factor,
    adapter_up_factor,
):
    count = lax.axis_size("dp")
    me, y = lax.axis_index("dp"), lax.axis_index("groups")
    z = me // 4
    own_rows, depth = tokens.shape
    total = own_rows * count
    width = gate_matrix.shape[1]
    rank = adapter_up_factor.shape[1]

    def swap(value, k):
        return lax.ppermute(value, "dp", [(d, d ^ k) for d in range(count)])

    def other(value):
        return lax.ppermute(value, "groups", [(0, 1), (1, 0)])

    ids = jnp.broadcast_to(token_adapter_index.astype(BF16), (own_rows, LANES))
    packed = jnp.concatenate([tokens, ids], axis=1)
    by_plane = [packed] + [swap(packed, 4 * j) for j in range(1, PLANES)]
    near = jnp.concatenate([p for q in by_plane for p in (q, swap(q, 2))], axis=0)
    far = swap(near, 1)

    pieces = repack(adapter_up_factor[0], width)
    stacks = []
    for k in range(len(CHUNKS)):
        own, core, cross, both = pieces[4 * k : 4 * k + 4]
        core = swap(core, 1)
        cross, both = swap(cross, 2), swap(both, 3)
        stacks.append((own, core, cross, other(cross), both, other(both)))

    place = jnp.arange(total, dtype=jnp.int32)
    block = place // own_rows
    distance = (block % 8) * 2 + block // 8
    order_of = (distance ^ me) * own_rows + place % own_rows
    all_ids = jnp.concatenate([near[:, depth], far[:, depth]]).astype(jnp.int32)
    adapters = jnp.arange(count, dtype=jnp.int32)
    slots = jnp.sum(jnp.where(all_ids[:, None] == adapters[None, :], adapter_slot_index[None, :], 0), 1)
    planes = slots // 4
    before = (planes[None, :] == planes[:, None]) & (order_of[None, :] < order_of[:, None])
    ranks = jnp.sum(before.astype(jnp.int32), 1)

    low = jnp.concatenate(
        [jnp.dot(v[:, :depth], adapter_down_factor[0], preferred_element_type=F32) for v in (near, far)], axis=0
    ).astype(BF16)
    mine = (slots == me)[None, :] & (ranks[None, :] == place[:, None])
    low = jnp.dot(mine.astype(BF16), low, preferred_element_type=F32).astype(BF16)

    def turned(v):
        return jnp.where(y == 0, v, jnp.concatenate([v[:, rank // 2 :], v[:, : rank // 2]], axis=1))

    e = jnp.concatenate([low, swap(low, 1), turned(swap(low, 2)), turned(swap(low, 3))], axis=1)

    rows_by_plane = {}
    for chunk, parts in zip(CHUNKS, stacks):
        for i, j in enumerate(chunk):
            out = delta_rows(e, parts, i, width)
            rows_by_plane[j] = swap(out, 4 * j) if j else out
    rows_by_plane = [rows_by_plane[j] for j in range(PLANES)]

    gate, up = base(near, far, gate_matrix, up_matrix)
    at = (planes ^ z) * total + ranks
    pick = (at[:, None] == jnp.arange(PLANES * total, dtype=jnp.int32)[None, :]).astype(BF16)
    order = (order_of[None, :] == place[:, None]).astype(BF16)
    return finish(gate, up, pick, order, rows_by_plane)


def solution(mesh):
    in_specs = (
        P(("groups", "dp"), None),
        P(("groups", "dp"), None),
        P(),
        P(None, "dp"),
        P(None, "dp"),
        P("dp", None, None),
        P("dp", None, None),
    )
    out_specs = P("groups", "dp")
    shards = plane_shards if mesh.shape["dp"] == 16 and mesh.shape["groups"] == 2 else general_shards
    return jax.shard_map(shards, mesh=mesh, in_specs=in_specs, out_specs=out_specs, check_vma=False)
```

```python
import functools

import jax
import jax.numpy as jnp
from jax import lax
from jax.experimental import pallas as pl
from jax.experimental.pallas import tpu as pltpu
from jax.sharding import PartitionSpec as P

CAP = 32
LANES = 128
PLANES = 4
F32 = jnp.float32
BF16 = jnp.bfloat16


def general_shards(
    tokens,
    token_adapter_index,
    adapter_slot_index,
    gate_matrix,
    up_matrix,
    adapter_down_factor,
    adapter_up_factor,
):
    count = lax.axis_size("dp")
    myself = lax.axis_index("dp")
    all_rows, all_ids = (
        lax.all_gather(tokens, "dp", axis=0, tiled=True),
        lax.all_gather(token_adapter_index, "dp", axis=0, tiled=True),
    )
    total = all_rows.shape[0]
    places = jnp.arange(count, dtype=jnp.int32)
    match = all_ids[:, 0][:, None] == places[None, :]
    slots = jnp.sum(jnp.where(match, adapter_slot_index[None, :], 0), 1)
    slot_match = slots[:, None] == places[None, :]
    onehot = slot_match.astype(jnp.int32)
    ranks = jnp.sum(jnp.cumsum(onehot, 0) * onehot, 1) - 1
    capacity = CAP
    columns = jnp.arange(capacity, dtype=jnp.int32)
    mine = (slots == myself)[:, None] & (ranks[:, None] == columns[None, :])
    row_list = jnp.sum(jnp.where(mine, jnp.arange(total, dtype=jnp.int32)[:, None], 0), 0)
    selected_slot = jnp.take(all_rows, row_list, axis=0)
    reduced_rows = jnp.dot(
        selected_slot, adapter_down_factor[0], preferred_element_type=F32
    ).astype(BF16)
    slot_pieces = lax.all_to_all(adapter_up_factor, "dp", split_axis=2, concat_axis=0, tiled=True)
    all_low = lax.all_gather(reduced_rows, "dp", axis=0, tiled=True)
    rank_width = all_low.shape[1]
    token_low = jnp.take(all_low, slots * capacity + ranks, axis=0)
    expanded = (token_low[:, None, :] * slot_match.astype(BF16)[:, :, None]).reshape(
        total, count * rank_width
    )
    stacked = slot_pieces.reshape(count * rank_width, slot_pieces.shape[2])
    delta = jnp.dot(expanded, stacked, preferred_element_type=F32).astype(BF16)
    gate_base = jnp.dot(all_rows, gate_matrix, preferred_element_type=F32)
    up = jnp.dot(all_rows, up_matrix, preferred_element_type=F32)
    gate = gate_base + delta.astype(F32)
    return (jax.nn.silu(gate) * up).astype(BF16)


ANY = pl.BlockSpec(memory_space=pl.ANY)
VMEM = pl.BlockSpec(memory_space=pltpu.VMEM)
CHUNKS = ((2, 3), (1, 0))
ROOM = 64


def repack_kernel(width, u_ref, *refs):
    outs, (held, in_sems, out_sems) = refs[:-3], refs[-3:]
    half = u_ref.shape[0] // 2
    me, y = lax.axis_index("dp"), lax.axis_index("groups")
    z, x, c = me // 4, (me // 2) % 2, me % 2
    ins, sends = [], []
    for k, chunk in enumerate(CHUNKS):
        own, core, cross, both = outs[4 * k : 4 * k + 4]
        for ref, xx, cc, split in (
            (cross, 1 - x, c, True),
            (both, 1 - x, 1 - c, True),
            (core, x, 1 - c, False),
            (own, x, c, False),
        ):
            for i, j in enumerate(chunk):
                zz = lax.bitwise_xor(z, j)
                n = len(ins)
                at = pl.multiple_of(((zz * 2 + xx) * 2 + cc) * width, LANES)
                rows = pl.ds(pl.multiple_of(y * half, half), half) if split else pl.ds(0, 2 * half)
                here = held.at[pl.ds(0, half if split else 2 * half), pl.ds(n * width, width)]
                ins.append(pltpu.make_async_copy(u_ref.at[rows, pl.ds(at, width)], here, in_sems.at[n]))
                sends.append(
                    pltpu.make_async_copy(here, ref.at[:, pl.ds(i * width, width)], out_sems.at[n])
                )
    for copy in ins:
        copy.start()
    for copy, send in zip(ins, sends):
        copy.wait()
        send.start()
    for send in sends:
        send.wait()


def repack(u, width):
    rank = u.shape[0]
    shapes = []
    for chunk in CHUNKS:
        n = len(chunk) * width
        shapes += [
            jax.ShapeDtypeStruct((rank, n), BF16),
            jax.ShapeDtypeStruct((rank, n), BF16),
            jax.ShapeDtypeStruct((rank // 2, n), BF16),
            jax.ShapeDtypeStruct((rank // 2, n), BF16),
        ]
    return pl.pallas_call(
        functools.partial(repack_kernel, width),
        out_shape=shapes,
        in_specs=[ANY],
        out_specs=[ANY] * len(shapes),
        scratch_shapes=[
            pltpu.VMEM((rank, 16 * width), BF16),
            pltpu.SemaphoreType.DMA((16,)),
            pltpu.SemaphoreType.DMA((16,)),
        ],
        compiler_params=pltpu.CompilerParams(vmem_limit_bytes=16 * 1024 * 1024),
        cost_estimate=pl.CostEstimate(flops=0, bytes_accessed=3 * u.size, transcendentals=0),
        name="repack",
    )(u)


def delta_kernel(width, e_ref, *refs):
    parts, outs = refs[:6], refs[6:]
    for i, out in enumerate(outs):
        stacked = jnp.concatenate([ref[:, i * width : (i + 1) * width] for ref in parts], axis=0)
        out[...] = jnp.dot(e_ref[...], stacked, preferred_element_type=F32).astype(BF16)


def delta_rows(e, parts, width):
    rows = e.shape[0]
    n = parts[0].shape[1] // width
    return pl.pallas_call(
        functools.partial(delta_kernel, width),
        out_shape=[jax.ShapeDtypeStruct((rows, width), BF16)] * n,
        in_specs=[VMEM] * (1 + len(parts)),
        out_specs=[VMEM] * n,
        compiler_params=pltpu.CompilerParams(vmem_limit_bytes=16 * 1024 * 1024),
        cost_estimate=pl.CostEstimate(
            flops=2 * rows * e.shape[1] * width * n,
            bytes_accessed=2 * n * width * (rows + e.shape[1]),
            transcendentals=0,
        ),
        name="delta_rows",
    )(e, *parts)


BLOCK = 512
SLOTS = 3


def base_kernel(first, steps, rows, more, *refs):
    x_refs, (g_ref, u_ref), refs = refs[:4], refs[4:6], refs[6:]
    sums, refs = (refs[:2], refs[2:]) if more else ((), refs)
    gate_ref, up_ref, x_held, g_held, u_held, x_sems, g_sems, u_sems = refs

    def weights(k, slot):
        at = pl.ds(pl.multiple_of((first + k) * BLOCK, BLOCK), BLOCK)
        return (
            pltpu.make_async_copy(g_ref.at[at], g_held.at[slot], g_sems.at[slot]),
            pltpu.make_async_copy(u_ref.at[at], u_held.at[slot], u_sems.at[slot]),
        )

    columns = pl.ds(first * BLOCK, steps * BLOCK)
    loads = [
        pltpu.make_async_copy(ref.at[:, columns], x_held.at[pl.ds(i * rows, rows)], x_sems.at[i])
        for i, ref in enumerate(x_refs)
    ]
    for copy in loads:
        copy.start()
    for k in range(min(SLOTS, steps)):
        for copy in weights(k, k):
            copy.start()
    gate_ref[...] = sums[0][...] if more else jnp.zeros_like(gate_ref)
    up_ref[...] = sums[1][...] if more else jnp.zeros_like(up_ref)
    for copy in loads:
        copy.wait()

    def step(k, carry):
        slot = lax.rem(k, SLOTS)
        gate_copy, up_copy = weights(k, slot)
        x = x_held[:, pl.ds(pl.multiple_of(k * BLOCK, BLOCK), BLOCK)]
        gate_copy.wait()
        gate_ref[...] += jnp.dot(x, g_held[slot], preferred_element_type=F32)
        up_copy.wait()
        up_ref[...] += jnp.dot(x, u_held[slot], preferred_element_type=F32)

        @pl.when(k + SLOTS < steps)
        def _():
            for copy in weights(k + SLOTS, slot):
                copy.start()

        return carry

    lax.fori_loop(0, steps, step, 0)


def base(x_parts, gate_matrix, up_matrix, first, steps, sums=()):
    width = gate_matrix.shape[1]
    rows = x_parts[0].shape[0]
    total = rows * len(x_parts)
    shape = jax.ShapeDtypeStruct((total, width), F32)
    return pl.pallas_call(
        functools.partial(base_kernel, first, steps, rows, bool(sums)),
        out_shape=[shape, shape],
        in_specs=[ANY] * (len(x_parts) + 2) + [VMEM] * len(sums),
        out_specs=[VMEM, VMEM],
        scratch_shapes=[
            pltpu.VMEM((total, steps * BLOCK), BF16),
            pltpu.VMEM((SLOTS, BLOCK, width), BF16),
            pltpu.VMEM((SLOTS, BLOCK, width), BF16),
            pltpu.SemaphoreType.DMA((len(x_parts),)),
            pltpu.SemaphoreType.DMA((SLOTS,)),
            pltpu.SemaphoreType.DMA((SLOTS,)),
        ],
        compiler_params=pltpu.CompilerParams(vmem_limit_bytes=32 * 1024 * 1024),
        cost_estimate=pl.CostEstimate(
            flops=4 * total * steps * BLOCK * width, bytes_accessed=4 * steps * BLOCK * width, transcendentals=0
        ),
        name="base",
    )(*x_parts, gate_matrix, up_matrix, *sums)


def finish_kernel(gate_ref, up_ref, pick_ref, order_ref, *refs):
    stacked = jnp.concatenate([ref[...] for ref in refs[:-1]], axis=0)
    delta = jnp.dot(pick_ref[...], stacked, preferred_element_type=F32)
    gate = gate_ref[...] + delta
    hidden = (gate / (1.0 + jnp.exp(-gate)) * up_ref[...]).astype(BF16)
    refs[-1][...] = jnp.dot(order_ref[...], hidden, preferred_element_type=F32).astype(BF16)


def finish(gate, up, pick, order, rows_by_plane):
    total, width = gate.shape
    step = width // 2 if width % (2 * LANES) == 0 else width
    col = lambda a: pl.BlockSpec((a.shape[0], step), lambda i: (0, i))
    whole = lambda a: pl.BlockSpec(a.shape, lambda i: (0, 0))
    return pl.pallas_call(
        finish_kernel,
        out_shape=jax.ShapeDtypeStruct((total, width), BF16),
        grid=(width // step,),
        in_specs=[col(gate), col(up), whole(pick), whole(order)] + [col(r) for r in rows_by_plane],
        out_specs=pl.BlockSpec((total, step), lambda i: (0, i)),
        compiler_params=pltpu.CompilerParams(vmem_limit_bytes=32 * 1024 * 1024),
        cost_estimate=pl.CostEstimate(flops=0, bytes_accessed=4 * total * width * 4, transcendentals=total * width),
        name="finish",
    )(gate, up, pick, order, *rows_by_plane)


def plane_shards(
    tokens,
    token_adapter_index,
    adapter_slot_index,
    gate_matrix,
    up_matrix,
    adapter_down_factor,
    adapter_up_factor,
):
    count = lax.axis_size("dp")
    me, y = lax.axis_index("dp"), lax.axis_index("groups")
    z = me // 4
    own_rows, depth = tokens.shape
    total = own_rows * count
    width = gate_matrix.shape[1]
    rank = adapter_up_factor.shape[1]

    def swap(value, k):
        return lax.ppermute(value, "dp", [(d, d ^ k) for d in range(count)])

    def other(value):
        return lax.ppermute(value, "groups", [(0, 1), (1, 0)])

    ids = jnp.broadcast_to(token_adapter_index.astype(BF16), (own_rows, LANES))
    packed = jnp.concatenate([tokens, ids], axis=1)
    by_plane = [packed] + [swap(packed, 4 * j) for j in range(1, PLANES)]
    near = [
        jnp.concatenate([p for q in by_plane[i : i + 2] for p in (q, swap(q, 2))], axis=0) for i in (0, 2)
    ]
    x_parts = (*near, *[swap(v, 1) for v in near])

    pieces = repack(adapter_up_factor[0], width)
    stacks = []
    for k in range(len(CHUNKS)):
        own, core, cross, both = pieces[4 * k : 4 * k + 4]
        cross, both = swap(cross, 2), swap(both, 3)
        stacks.append((own, swap(core, 1), cross, other(cross), both, other(both)))

    place = jnp.arange(total, dtype=jnp.int32)
    block = place // own_rows
    distance = (block % 8) * 2 + block // 8
    order_of = (distance ^ me) * own_rows + place % own_rows
    all_ids = jnp.concatenate([v[:, depth] for v in x_parts]).astype(jnp.int32)
    adapters = jnp.arange(count, dtype=jnp.int32)
    slots = jnp.sum(jnp.where(all_ids[:, None] == adapters[None, :], adapter_slot_index[None, :], 0), 1)
    planes = slots // 4
    before = (planes[None, :] == planes[:, None]) & (order_of[None, :] < order_of[:, None])
    ranks = jnp.sum(before.astype(jnp.int32), 1)
    most = jnp.max(ranks)
    all_most = jnp.maximum(most, jnp.max(other(jnp.broadcast_to(most, (8, LANES)))))

    low = jnp.concatenate(
        [jnp.dot(v[:, :depth], adapter_down_factor[0], preferred_element_type=F32) for v in x_parts], axis=0
    ).astype(BF16)
    mine = (slots == me)[None, :] & (ranks[None, :] == place[:, None])
    low = jnp.dot(mine.astype(BF16), low, preferred_element_type=F32).astype(BF16)
    low, x_parts = lax.optimization_barrier((low, x_parts))

    def turned(v):
        return jnp.where(y == 0, v, jnp.concatenate([v[:, rank // 2 :], v[:, : rank // 2]], axis=1))

    lows = [low, swap(low, 1), swap(low, 2), swap(low, 3)]
    steps = depth // BLOCK
    early = steps // 4
    sums = base(x_parts, gate_matrix, up_matrix, 0, early)
    lows, sums = lax.optimization_barrier((lows, sums))
    e = jnp.concatenate([lows[0], lows[1], turned(lows[2]), turned(lows[3])], axis=1)

    def rows_of(e):
        by_plane = {}
        for chunk, parts in zip(CHUNKS, stacks):
            by_plane.update(zip(chunk, delta_rows(e, parts, width)))
        return [by_plane[j] for j in range(PLANES)]

    def sent(rows):
        return [rows[0]] + [swap(rows[j], 4 * j) for j in (1, 2, 3)]

    rows, sums = lax.optimization_barrier((rows_of(e[:ROOM]), sums))
    rows = sent(rows)
    gate, up = base(x_parts, gate_matrix, up_matrix, early, steps - early, sums)

    order = (order_of[None, :] == place[:, None]).astype(BF16)
    plane = planes ^ z

    def picked(room, start):
        at = jnp.where((ranks >= start) & (ranks < start + room), plane * room + ranks - start, -1)
        return (at[:, None] == jnp.arange(PLANES * room, dtype=jnp.int32)[None, :]).astype(BF16)

    first = picked(ROOM, 0)

    def short():
        return finish(gate, up, first, order, rows)

    def long():
        rest = sent(rows_of(e[ROOM:]))
        pick = jnp.concatenate([first, picked(total - ROOM, ROOM)], axis=1)
        return finish(gate, up, pick, order, rows + rest)

    return lax.cond(all_most < ROOM, short, long)


def solution(mesh):
    in_specs = (
        P(("groups", "dp"), None),
        P(("groups", "dp"), None),
        P(),
        P(None, "dp"),
        P(None, "dp"),
        P("dp", None, None),
        P("dp", None, None),
    )
    out_specs = P("groups", "dp")
    shards = plane_shards if mesh.shape["dp"] == 16 and mesh.shape["groups"] == 2 else general_shards
    return jax.shard_map(shards, mesh=mesh, in_specs=in_specs, out_specs=out_specs, check_vma=False)
```

```python
import functools

import jax
import jax.numpy as jnp
from jax import lax
from jax.experimental import pallas as pl
from jax.experimental.pallas import tpu as pltpu
from jax.sharding import PartitionSpec as P

CAP = 32
LANES = 128
PLANES = 4
F32 = jnp.float32
BF16 = jnp.bfloat16


def general_shards(
    tokens,
    token_adapter_index,
    adapter_slot_index,
    gate_matrix,
    up_matrix,
    adapter_down_factor,
    adapter_up_factor,
):
    count = lax.axis_size("dp")
    myself = lax.axis_index("dp")
    all_rows, all_ids = (
        lax.all_gather(tokens, "dp", axis=0, tiled=True),
        lax.all_gather(token_adapter_index, "dp", axis=0, tiled=True),
    )
    total = all_rows.shape[0]
    places = jnp.arange(count, dtype=jnp.int32)
    match = all_ids[:, 0][:, None] == places[None, :]
    slots = jnp.sum(jnp.where(match, adapter_slot_index[None, :], 0), 1)
    slot_match = slots[:, None] == places[None, :]
    onehot = slot_match.astype(jnp.int32)
    ranks = jnp.sum(jnp.cumsum(onehot, 0) * onehot, 1) - 1
    capacity = CAP
    columns = jnp.arange(capacity, dtype=jnp.int32)
    mine = (slots == myself)[:, None] & (ranks[:, None] == columns[None, :])
    row_list = jnp.sum(jnp.where(mine, jnp.arange(total, dtype=jnp.int32)[:, None], 0), 0)
    selected_slot = jnp.take(all_rows, row_list, axis=0)
    reduced_rows = jnp.dot(
        selected_slot, adapter_down_factor[0], preferred_element_type=F32
    ).astype(BF16)
    slot_pieces = lax.all_to_all(adapter_up_factor, "dp", split_axis=2, concat_axis=0, tiled=True)
    all_low = lax.all_gather(reduced_rows, "dp", axis=0, tiled=True)
    rank_width = all_low.shape[1]
    token_low = jnp.take(all_low, slots * capacity + ranks, axis=0)
    expanded = (token_low[:, None, :] * slot_match.astype(BF16)[:, :, None]).reshape(
        total, count * rank_width
    )
    stacked = slot_pieces.reshape(count * rank_width, slot_pieces.shape[2])
    delta = jnp.dot(expanded, stacked, preferred_element_type=F32).astype(BF16)
    gate_base = jnp.dot(all_rows, gate_matrix, preferred_element_type=F32)
    up = jnp.dot(all_rows, up_matrix, preferred_element_type=F32)
    gate = gate_base + delta.astype(F32)
    return (jax.nn.silu(gate) * up).astype(BF16)


ANY = pl.BlockSpec(memory_space=pl.ANY)
VMEM = pl.BlockSpec(memory_space=pltpu.VMEM)
ROOMS = (64, 16, 48)
FACTORS = (2, 3)
ROWS = (0, 1)
BLOCKS = PLANES + len(ROWS)


def repack_kernel(width, u_ref, own_ref, core_ref, cross_ref, both_ref, held, in_sems, out_sems):
    rank = u_ref.shape[0]
    half = rank // 2
    me, y = lax.axis_index("dp"), lax.axis_index("groups")
    z, x, c = me // 4, (me // 2) % 2, me % 2
    ins, sends = [], []

    def move(j, xx, cc, split, target):
        n = len(ins)
        at = pl.multiple_of(((lax.bitwise_xor(z, j) * 2 + xx) * 2 + cc) * width, LANES)
        rows = pl.ds(pl.multiple_of(y * half, half), half) if split else pl.ds(0, rank)
        here = held.at[pl.ds(0, half if split else rank), pl.ds(n * width, width)]
        ins.append(pltpu.make_async_copy(u_ref.at[rows, pl.ds(at, width)], here, in_sems.at[n]))
        sends.append(pltpu.make_async_copy(here, target, out_sems.at[n]))

    for i, j in enumerate(FACTORS):
        move(j, 1 - x, c, True, cross_ref.at[:, pl.ds(i * width, width)])
        move(j, 1 - x, 1 - c, True, both_ref.at[:, pl.ds(i * width, width)])
    for cc, ref in ((1 - c, core_ref), (c, own_ref)):
        for i, (j, xx) in enumerate([(j, x) for j in range(PLANES)] + [(j, 1 - x) for j in ROWS]):
            move(j, xx, cc, False, ref.at[:, pl.ds(i * width, width)])
    for copy in ins:
        copy.start()
    for copy, send in zip(ins, sends):
        copy.wait()
        send.start()
    for send in sends:
        send.wait()


def repack(u, width):
    rank = u.shape[0]
    wide = jax.ShapeDtypeStruct((rank, BLOCKS * width), BF16)
    split = jax.ShapeDtypeStruct((rank // 2, len(FACTORS) * width), BF16)
    shapes = [wide, wide, split, split]
    return pl.pallas_call(
        functools.partial(repack_kernel, width),
        out_shape=shapes,
        in_specs=[ANY],
        out_specs=[ANY] * len(shapes),
        scratch_shapes=[
            pltpu.VMEM((rank, 16 * width), BF16),
            pltpu.SemaphoreType.DMA((16,)),
            pltpu.SemaphoreType.DMA((16,)),
        ],
        compiler_params=pltpu.CompilerParams(vmem_limit_bytes=16 * 1024 * 1024),
        cost_estimate=pl.CostEstimate(flops=0, bytes_accessed=3 * u.size, transcendentals=0),
        name="repack",
    )(u)


def delta_kernel(plan, width, e_ref, *refs):
    parts, outs = refs[: len(refs) - len(plan)], refs[len(refs) - len(plan) :]
    for pieces, out in zip(plan, outs):
        stacked = jnp.concatenate(
            [parts[n][:rows, i * width : (i + 1) * width] for n, i, rows in pieces], axis=0
        )
        out[...] = jnp.dot(e_ref[:, : stacked.shape[0]], stacked, preferred_element_type=F32).astype(BF16)


def delta_rows(e, parts, plan, width):
    rows = e.shape[0]
    n = len(plan)
    return pl.pallas_call(
        functools.partial(delta_kernel, plan, width),
        out_shape=[jax.ShapeDtypeStruct((rows, width), BF16)] * n,
        in_specs=[VMEM] * (1 + len(parts)),
        out_specs=[VMEM] * n,
        compiler_params=pltpu.CompilerParams(vmem_limit_bytes=16 * 1024 * 1024),
        cost_estimate=pl.CostEstimate(
            flops=2 * rows * e.shape[1] * width * n,
            bytes_accessed=2 * n * width * (rows + e.shape[1]),
            transcendentals=0,
        ),
        name="delta_rows",
    )(e, *parts)


BLOCK = 512
SLOTS = 3


def base_kernel(first, steps, rows, more, *refs):
    x_refs, (g_ref, u_ref), refs = refs[:4], refs[4:6], refs[6:]
    sums, refs = (refs[:2], refs[2:]) if more else ((), refs)
    gate_ref, up_ref, x_held, g_held, u_held, x_sems, g_sems, u_sems = refs

    def weights(k, slot):
        at = pl.ds(pl.multiple_of((first + k) * BLOCK, BLOCK), BLOCK)
        return (
            pltpu.make_async_copy(g_ref.at[at], g_held.at[slot], g_sems.at[slot]),
            pltpu.make_async_copy(u_ref.at[at], u_held.at[slot], u_sems.at[slot]),
        )

    columns = pl.ds(first * BLOCK, steps * BLOCK)
    loads = [
        pltpu.make_async_copy(ref.at[:, columns], x_held.at[pl.ds(i * rows, rows)], x_sems.at[i])
        for i, ref in enumerate(x_refs)
    ]
    for copy in loads:
        copy.start()
    for k in range(min(SLOTS, steps)):
        for copy in weights(k, k):
            copy.start()
    gate_ref[...] = sums[0][...] if more else jnp.zeros_like(gate_ref)
    up_ref[...] = sums[1][...] if more else jnp.zeros_like(up_ref)
    for copy in loads:
        copy.wait()

    def step(k, carry):
        slot = lax.rem(k, SLOTS)
        gate_copy, up_copy = weights(k, slot)
        x = x_held[:, pl.ds(pl.multiple_of(k * BLOCK, BLOCK), BLOCK)]
        gate_copy.wait()
        gate_ref[...] += jnp.dot(x, g_held[slot], preferred_element_type=F32)
        up_copy.wait()
        up_ref[...] += jnp.dot(x, u_held[slot], preferred_element_type=F32)

        @pl.when(k + SLOTS < steps)
        def _():
            for copy in weights(k + SLOTS, slot):
                copy.start()

        return carry

    lax.fori_loop(0, steps, step, 0)


def base(x_parts, gate_matrix, up_matrix, first, steps, sums=()):
    width = gate_matrix.shape[1]
    rows = x_parts[0].shape[0]
    total = rows * len(x_parts)
    shape = jax.ShapeDtypeStruct((total, width), F32)
    return pl.pallas_call(
        functools.partial(base_kernel, first, steps, rows, bool(sums)),
        out_shape=[shape, shape],
        in_specs=[ANY] * (len(x_parts) + 2) + [VMEM] * len(sums),
        out_specs=[VMEM, VMEM],
        scratch_shapes=[
            pltpu.VMEM((total, steps * BLOCK), BF16),
            pltpu.VMEM((SLOTS, BLOCK, width), BF16),
            pltpu.VMEM((SLOTS, BLOCK, width), BF16),
            pltpu.SemaphoreType.DMA((len(x_parts),)),
            pltpu.SemaphoreType.DMA((SLOTS,)),
            pltpu.SemaphoreType.DMA((SLOTS,)),
        ],
        compiler_params=pltpu.CompilerParams(vmem_limit_bytes=32 * 1024 * 1024),
        cost_estimate=pl.CostEstimate(
            flops=4 * total * steps * BLOCK * width, bytes_accessed=4 * steps * BLOCK * width, transcendentals=0
        ),
        name="base",
    )(*x_parts, gate_matrix, up_matrix, *sums)


def finish_kernel(gate_ref, up_ref, pick_ref, order_ref, *refs):
    stacked = jnp.concatenate([ref[...] for ref in refs[:-1]], axis=0)
    delta = jnp.dot(pick_ref[...], stacked, preferred_element_type=F32)
    gate = gate_ref[...] + delta
    hidden = (gate / (1.0 + jnp.exp(-gate)) * up_ref[...]).astype(BF16)
    refs[-1][...] = jnp.dot(order_ref[...], hidden, preferred_element_type=F32).astype(BF16)


def finish(gate, up, pick, order, rows_by_plane):
    total, width = gate.shape
    step = width // 2 if width % (2 * LANES) == 0 else width
    col = lambda a: pl.BlockSpec((a.shape[0], step), lambda i: (0, i))
    whole = lambda a: pl.BlockSpec(a.shape, lambda i: (0, 0))
    return pl.pallas_call(
        finish_kernel,
        out_shape=jax.ShapeDtypeStruct((total, width), BF16),
        grid=(width // step,),
        in_specs=[col(gate), col(up), whole(pick), whole(order)] + [col(r) for r in rows_by_plane],
        out_specs=pl.BlockSpec((total, step), lambda i: (0, i)),
        compiler_params=pltpu.CompilerParams(vmem_limit_bytes=32 * 1024 * 1024),
        cost_estimate=pl.CostEstimate(flops=0, bytes_accessed=4 * total * width * 4, transcendentals=total * width),
        name="finish",
    )(gate, up, pick, order, *rows_by_plane)


def plane_shards(
    tokens,
    token_adapter_index,
    adapter_slot_index,
    gate_matrix,
    up_matrix,
    adapter_down_factor,
    adapter_up_factor,
):
    count = lax.axis_size("dp")
    me, y = lax.axis_index("dp"), lax.axis_index("groups")
    z = me // 4
    own_rows, depth = tokens.shape
    total = own_rows * count
    width = gate_matrix.shape[1]
    rank = adapter_up_factor.shape[1]

    def swap(value, k):
        return lax.ppermute(value, "dp", [(d, d ^ k) for d in range(count)])

    def other(value):
        return lax.ppermute(value, "groups", [(0, 1), (1, 0)])

    ids = jnp.broadcast_to(token_adapter_index.astype(BF16), (own_rows, LANES))
    packed = jnp.concatenate([tokens, ids], axis=1)
    second, third = swap(packed, 8), swap(packed, 12)
    pair = jnp.concatenate([packed, swap(packed, 2)], axis=0)
    close = jnp.concatenate([pair, swap(pair, 4)], axis=0)
    remote = jnp.concatenate([second, third], axis=0)
    remote = jnp.concatenate([remote, swap(remote, 2)], axis=0)
    x_parts = (close, remote, swap(close, 1), swap(remote, 1))
    distances = [0, 2, 4, 6, 8, 12, 10, 14]
    distances = distances + [k + 1 for k in distances]

    own, core, cross, both = repack(adapter_up_factor[0], width)
    core = swap(core, 1)
    cross, both = swap(cross, 2), swap(both, 3)
    cross_parts = (cross, other(cross), both, other(both))
    half = rank // 2

    place = jnp.arange(total, dtype=jnp.int32)
    order_of = (jnp.repeat(jnp.array(distances, jnp.int32), own_rows) ^ me) * own_rows + place % own_rows
    all_ids = jnp.concatenate([v[:, depth] for v in x_parts]).astype(jnp.int32)
    adapters = jnp.arange(count, dtype=jnp.int32)
    slots = jnp.sum(jnp.where(all_ids[:, None] == adapters[None, :], adapter_slot_index[None, :], 0), 1)
    planes = slots // 4
    before = (planes[None, :] == planes[:, None]) & (order_of[None, :] < order_of[:, None])
    ranks = jnp.sum(before.astype(jnp.int32), 1)

    low = jnp.concatenate(
        [jnp.dot(v[:, :depth], adapter_down_factor[0], preferred_element_type=F32) for v in x_parts], axis=0
    ).astype(BF16)
    mine = ((slots == me)[None, :] & (ranks[None, :] == place[:, None])).astype(BF16)
    low = jnp.dot(mine, low, preferred_element_type=F32).astype(BF16)
    low, x_parts, slots, ranks = lax.optimization_barrier((low, x_parts, slots, ranks))

    def turned(v):
        return jnp.where(y == 0, v, jnp.concatenate([v[:, half:], v[:, :half]], axis=1))

    chip = jnp.concatenate([low, swap(low, 1)], axis=1)
    plane = jnp.concatenate([chip, turned(swap(low, 2)), turned(swap(low, 3))], axis=1)
    chip_plan = tuple(((0, i, rank), (1, i, rank)) for i in (0, 1, PLANES, PLANES + 1))
    plane_plan = tuple(
        ((0, j, rank), (1, j, rank)) + tuple((n, i, half) for n in (2, 3, 4, 5)) for i, j in enumerate(FACTORS)
    )

    def sent(start, room):
        at = slice(start, start + room)
        here, first, here_cross, first_cross = delta_rows(chip[at], (own, core), chip_plan, width)
        second, third = delta_rows(plane[at], (own, core, *cross_parts), plane_plan, width)
        return here, first, second, third, here_cross, first_cross

    def arrived(rows):
        return [rows[0]] + [swap(v, k) for v, k in zip(rows[1:], (4, 8, 12, 2, 6))]

    rows, x_parts = lax.optimization_barrier((sent(0, ROOMS[0]), x_parts))
    rows = arrived(rows)
    gate, up = base(x_parts, gate_matrix, up_matrix, 0, depth // BLOCK)

    order = (order_of[None, :] == place[:, None]).astype(BF16)
    most = jnp.max(ranks) + 1
    most = jnp.maximum(most, jnp.max(other(jnp.broadcast_to(most, (8, LANES)))))
    branch = (most > ROOMS[0]).astype(jnp.int32) + (most > ROOMS[0] + ROOMS[1]).astype(jnp.int32)

    def picked(start, room):
        at = jnp.where((ranks >= start) & (ranks < start + room), ((slots // 4) ^ z) * room + ranks - start, -1)
        pick = (at[:, None] == jnp.arange(PLANES * room, dtype=jnp.int32)[None, :]).astype(BF16)
        return jnp.concatenate([pick, pick[:, : len(ROWS) * room]], axis=1)

    first = picked(0, ROOMS[0])

    def short():
        return finish(gate, up, first, order, rows)

    def more(room):
        rest = arrived(sent(ROOMS[0], room))
        pick = jnp.concatenate([first, picked(ROOMS[0], room)], axis=1)
        return finish(gate, up, pick, order, rows + rest)

    return lax.switch(branch, (short, lambda: more(ROOMS[1]), lambda: more(ROOMS[1] + ROOMS[2])))


def solution(mesh):
    in_specs = (
        P(("groups", "dp"), None),
        P(("groups", "dp"), None),
        P(),
        P(None, "dp"),
        P(None, "dp"),
        P("dp", None, None),
        P("dp", None, None),
    )
    out_specs = P("groups", "dp")
    shards = plane_shards if mesh.shape["dp"] == 16 and mesh.shape["groups"] == 2 else general_shards
    return jax.shard_map(shards, mesh=mesh, in_specs=in_specs, out_specs=out_specs, check_vma=False)
```

```python
import functools

import jax
import jax.numpy as jnp
from jax import lax
from jax.experimental import pallas as pl
from jax.experimental.pallas import tpu as pltpu
from jax.sharding import PartitionSpec as P

CAP = 32
LANES = 128
PLANES = 4
F32 = jnp.float32
BF16 = jnp.bfloat16


def general_shards(
    tokens,
    token_adapter_index,
    adapter_slot_index,
    gate_matrix,
    up_matrix,
    adapter_down_factor,
    adapter_up_factor,
):
    count = lax.axis_size("dp")
    myself = lax.axis_index("dp")
    all_rows, all_ids = (
        lax.all_gather(tokens, "dp", axis=0, tiled=True),
        lax.all_gather(token_adapter_index, "dp", axis=0, tiled=True),
    )
    total = all_rows.shape[0]
    places = jnp.arange(count, dtype=jnp.int32)
    match = all_ids[:, 0][:, None] == places[None, :]
    slots = jnp.sum(jnp.where(match, adapter_slot_index[None, :], 0), 1)
    slot_match = slots[:, None] == places[None, :]
    onehot = slot_match.astype(jnp.int32)
    ranks = jnp.sum(jnp.cumsum(onehot, 0) * onehot, 1) - 1
    capacity = CAP
    columns = jnp.arange(capacity, dtype=jnp.int32)
    mine = (slots == myself)[:, None] & (ranks[:, None] == columns[None, :])
    row_list = jnp.sum(jnp.where(mine, jnp.arange(total, dtype=jnp.int32)[:, None], 0), 0)
    selected_slot = jnp.take(all_rows, row_list, axis=0)
    reduced_rows = jnp.dot(
        selected_slot, adapter_down_factor[0], preferred_element_type=F32
    ).astype(BF16)
    slot_pieces = lax.all_to_all(adapter_up_factor, "dp", split_axis=2, concat_axis=0, tiled=True)
    all_low = lax.all_gather(reduced_rows, "dp", axis=0, tiled=True)
    rank_width = all_low.shape[1]
    token_low = jnp.take(all_low, slots * capacity + ranks, axis=0)
    expanded = (token_low[:, None, :] * slot_match.astype(BF16)[:, :, None]).reshape(
        total, count * rank_width
    )
    stacked = slot_pieces.reshape(count * rank_width, slot_pieces.shape[2])
    delta = jnp.dot(expanded, stacked, preferred_element_type=F32).astype(BF16)
    gate_base = jnp.dot(all_rows, gate_matrix, preferred_element_type=F32)
    up = jnp.dot(all_rows, up_matrix, preferred_element_type=F32)
    gate = gate_base + delta.astype(F32)
    return (jax.nn.silu(gate) * up).astype(BF16)


ANY = pl.BlockSpec(memory_space=pl.ANY)
HBM = pl.BlockSpec(memory_space=pltpu.HBM)
VMEM = pl.BlockSpec(memory_space=pltpu.VMEM)
ROOMS = (64, 16, 48)
FACTORS = (2, 3)
ROWS = (0, 1)


def cut(u_ref, held, in_sems, out_sems, width, wanted):
    rank = u_ref.shape[0]
    half = rank // 2
    z = lax.axis_index("dp") // 4
    ins, sends = [], []
    for n, (j, x, c, part, target) in enumerate(wanted):
        at = pl.multiple_of(((lax.bitwise_xor(z, j) * 2 + x) * 2 + c) * width, LANES)
        rows = pl.ds(0, rank) if part is None else pl.ds(pl.multiple_of(part * half, half), half)
        here = held.at[pl.ds(0, rank if part is None else half), pl.ds(n * width, width)]
        ins.append(pltpu.make_async_copy(u_ref.at[rows, pl.ds(at, width)], here, in_sems.at[n]))
        sends.append(pltpu.make_async_copy(here, target, out_sems.at[n]))
    for copy in ins:
        copy.start()
    for copy, send in zip(ins, sends):
        copy.wait()
        send.start()
    for send in sends:
        send.wait()


def position():
    me = lax.axis_index("dp")
    return (me // 2) % 2, me % 2


def cross_kernel(width, u_ref, cross_ref, both_ref, *scratch):
    (x, c), y = position(), lax.axis_index("groups")
    wanted = []
    for i, j in enumerate(FACTORS):
        place = pl.ds(i * width, width)
        wanted += [(j, 1 - x, c, y, cross_ref.at[:, place]), (j, 1 - x, 1 - c, y, both_ref.at[:, place])]
    cut(u_ref, *scratch, width, wanted)


def cut_cross(u, width):
    rank = u.shape[0]
    n = 2 * len(FACTORS)
    split = jax.ShapeDtypeStruct((rank // 2, len(FACTORS) * width), BF16)
    return pl.pallas_call(
        functools.partial(cross_kernel, width),
        out_shape=[split, split],
        in_specs=[HBM],
        out_specs=[ANY, ANY],
        scratch_shapes=[
            pltpu.VMEM((rank // 2, n * width), BF16),
            pltpu.SemaphoreType.DMA((n,)),
            pltpu.SemaphoreType.DMA((n,)),
        ],
        compiler_params=pltpu.CompilerParams(vmem_limit_bytes=61 * 1024 * 1024),
        cost_estimate=pl.CostEstimate(flops=0, bytes_accessed=2 * rank * n * width, transcendentals=0),
        name="cut_cross",
    )(u)


def repack_kernel(width, u_ref, own_rows_ref, own_ref, core_rows_ref, core_ref, *scratch):
    x, c = position()
    wanted = []
    for cc, rows_ref, ref in ((1 - c, core_rows_ref, core_ref), (c, own_rows_ref, own_ref)):
        for target, blocks in (
            (ref, [(j, x) for j in FACTORS]),
            (rows_ref, [(j, xx) for xx in (x, 1 - x) for j in ROWS]),
        ):
            for i, (j, xx) in enumerate(blocks):
                wanted.append((j, xx, cc, None, target.at[:, pl.ds(i * width, width)]))
    cut(u_ref, *scratch, width, wanted)


def repack(u, width):
    rank = u.shape[0]
    n = 2 * (len(FACTORS) + 2 * len(ROWS))
    for_rows = jax.ShapeDtypeStruct((rank, 2 * len(ROWS) * width), BF16)
    for_factors = jax.ShapeDtypeStruct((rank, len(FACTORS) * width), BF16)
    return pl.pallas_call(
        functools.partial(repack_kernel, width),
        out_shape=[for_rows, for_factors] * 2,
        in_specs=[HBM],
        out_specs=[ANY] * 4,
        scratch_shapes=[
            pltpu.VMEM((rank, n * width), BF16),
            pltpu.SemaphoreType.DMA((n,)),
            pltpu.SemaphoreType.DMA((n,)),
        ],
        compiler_params=pltpu.CompilerParams(vmem_limit_bytes=61 * 1024 * 1024),
        cost_estimate=pl.CostEstimate(flops=0, bytes_accessed=3 * u.size, transcendentals=0),
        name="repack",
    )(u)


def low_kernel(*refs):
    x_refs, (down_ref, table_ref, at_ref, at_column_ref), outs = refs[:4], refs[4:8], refs[8:]
    low_ref, meta_ref, pick_ref, order_ref, rounds_ref = outs
    depth = down_ref.shape[1]
    x = jnp.concatenate([ref[:, :depth] for ref in x_refs], axis=0)
    low = lax.dot_general(x, down_ref[...], (((1,), (1,)), ((), ())), preferred_element_type=F32).astype(BF16)
    ids = jnp.concatenate([ref[:, depth:] for ref in x_refs], axis=0).astype(F32)
    total = ids.shape[0]
    lane = lax.broadcasted_iota(jnp.int32, ids.shape, 1).astype(F32)
    place = lax.broadcasted_iota(jnp.int32, ids.shape, 0).astype(F32)
    table = jnp.broadcast_to(table_ref[...], ids.shape).astype(F32)
    slots = jnp.broadcast_to(jnp.sum(jnp.where(ids == lane, table, 0.0), axis=1, keepdims=True), (total, total))
    slots_row = slots.T
    planes, planes_row = jnp.floor(slots * 0.25), jnp.floor(slots_row * 0.25)
    at = jnp.broadcast_to(at_ref[...], ids.shape).astype(F32)
    at_column = jnp.broadcast_to(at_column_ref[...], ids.shape).astype(F32)
    same = planes == planes_row
    ranks_row = jnp.sum(jnp.where(same & (at_column < at), 1.0, 0.0), axis=0, keepdims=True)
    ranks = jnp.sum(jnp.where(same & (at < at_column), 1.0, 0.0), axis=1, keepdims=True)
    me = lax.axis_index("dp")
    mine = jnp.where((slots_row == me.astype(F32)) & (ranks_row == place), 1.0, 0.0).astype(BF16)
    low_ref[...] = jnp.dot(mine, low, preferred_element_type=F32).astype(BF16)
    meta_ref[0:1, :] = slots_row[0:1, :].astype(jnp.int32)
    meta_ref[1:2, :] = ranks_row.astype(jnp.int32)
    order_ref[...] = jnp.where(at == place, 1.0, 0.0).astype(BF16)
    room = ROOMS[0]
    wide = lax.broadcasted_iota(jnp.int32, pick_ref.shape, 1)
    block = wide // room
    distance = jnp.where(block < PLANES, block, block - PLANES)
    wanted = lax.bitwise_xor(distance, jnp.broadcast_to(me // 4, distance.shape)).astype(F32)
    found = (planes[:, :1] == wanted) & (ranks == (wide % room).astype(F32))
    pick_ref[...] = jnp.where(found, 1.0, 0.0).astype(BF16)
    most = jnp.max(ranks_row)
    rounds_ref[0] = (most >= room).astype(jnp.int32) + (most >= room + ROOMS[1]).astype(jnp.int32)


def low_rows(x_parts, down, table, order_of):
    total = order_of.shape[0]
    rank = down.shape[0]
    return pl.pallas_call(
        low_kernel,
        out_shape=[
            jax.ShapeDtypeStruct((total, rank), BF16),
            jax.ShapeDtypeStruct((2, total), jnp.int32),
            jax.ShapeDtypeStruct((total, (PLANES + len(ROWS)) * ROOMS[0]), BF16),
            jax.ShapeDtypeStruct((total, total), BF16),
            jax.ShapeDtypeStruct((1,), jnp.int32),
        ],
        in_specs=[VMEM] * 8,
        out_specs=[VMEM] * 4 + [pl.BlockSpec(memory_space=pltpu.SMEM)],
        compiler_params=pltpu.CompilerParams(vmem_limit_bytes=16 * 1024 * 1024),
        cost_estimate=pl.CostEstimate(flops=0, bytes_accessed=60 * 1024 * 1024, transcendentals=0),
        name="low_rows",
    )(*x_parts, down, table, order_of[None, :], order_of[:, None])


def delta_kernel(plan, width, e_ref, *refs):
    parts, outs = refs[: len(refs) - len(plan)], refs[len(refs) - len(plan) :]
    for pieces, out in zip(plan, outs):
        stacked = jnp.concatenate(
            [parts[n][at : at + rows, i * width : (i + 1) * width] for n, i, at, rows in pieces], axis=0
        )
        out[...] = jnp.dot(e_ref[:, : stacked.shape[0]], stacked, preferred_element_type=F32).astype(BF16)


def delta_rows(e, parts, plan, width):
    rows = e.shape[0]
    n = len(plan)
    return pl.pallas_call(
        functools.partial(delta_kernel, plan, width),
        out_shape=[jax.ShapeDtypeStruct((rows, width), BF16)] * n,
        in_specs=[VMEM] * (1 + len(parts)),
        out_specs=[VMEM] * n,
        compiler_params=pltpu.CompilerParams(vmem_limit_bytes=8 * 1024 * 1024),
        cost_estimate=pl.CostEstimate(
            flops=2 * rows * e.shape[1] * width * n,
            bytes_accessed=2 * n * width * (rows + e.shape[1]),
            transcendentals=0,
        ),
        name="delta_rows",
    )(e, *parts)


BLOCK = 512
SLOTS = 3


def base_kernel(first, steps, rows, more, *refs):
    x_refs, (g_ref, u_ref), refs = refs[:4], refs[4:6], refs[6:]
    sums, refs = (refs[:2], refs[2:]) if more else ((), refs)
    gate_ref, up_ref, x_held, g_held, u_held, x_sems, g_sems, u_sems = refs

    def weights(k, slot):
        at = pl.ds(pl.multiple_of((first + k) * BLOCK, BLOCK), BLOCK)
        return (
            pltpu.make_async_copy(g_ref.at[at], g_held.at[slot], g_sems.at[slot]),
            pltpu.make_async_copy(u_ref.at[at], u_held.at[slot], u_sems.at[slot]),
        )

    columns = pl.ds(first * BLOCK, steps * BLOCK)
    loads = [
        pltpu.make_async_copy(ref.at[:, columns], x_held.at[pl.ds(i * rows, rows)], x_sems.at[i])
        for i, ref in enumerate(x_refs)
    ]
    for copy in loads:
        copy.start()
    for k in range(min(SLOTS, steps)):
        for copy in weights(k, k):
            copy.start()
    gate_ref[...] = sums[0][...] if more else jnp.zeros_like(gate_ref)
    up_ref[...] = sums[1][...] if more else jnp.zeros_like(up_ref)
    for copy in loads:
        copy.wait()

    def step(k, carry):
        slot = lax.rem(k, SLOTS)
        gate_copy, up_copy = weights(k, slot)
        x = x_held[:, pl.ds(pl.multiple_of(k * BLOCK, BLOCK), BLOCK)]
        gate_copy.wait()
        gate_ref[...] += jnp.dot(x, g_held[slot], preferred_element_type=F32)
        up_copy.wait()
        up_ref[...] += jnp.dot(x, u_held[slot], preferred_element_type=F32)

        @pl.when(k + SLOTS < steps)
        def _():
            for copy in weights(k + SLOTS, slot):
                copy.start()

        return carry

    lax.fori_loop(0, steps, step, 0)


def base(x_parts, gate_matrix, up_matrix, first, steps, sums=()):
    width = gate_matrix.shape[1]
    rows = x_parts[0].shape[0]
    total = rows * len(x_parts)
    shape = jax.ShapeDtypeStruct((total, width), F32)
    return pl.pallas_call(
        functools.partial(base_kernel, first, steps, rows, bool(sums)),
        out_shape=[shape, shape],
        in_specs=[ANY] * len(x_parts) + [HBM] * 2 + [VMEM] * len(sums),
        out_specs=[VMEM, VMEM],
        scratch_shapes=[
            pltpu.VMEM((total, steps * BLOCK), BF16),
            pltpu.VMEM((SLOTS, BLOCK, width), BF16),
            pltpu.VMEM((SLOTS, BLOCK, width), BF16),
            pltpu.SemaphoreType.DMA((len(x_parts),)),
            pltpu.SemaphoreType.DMA((SLOTS,)),
            pltpu.SemaphoreType.DMA((SLOTS,)),
        ],
        compiler_params=pltpu.CompilerParams(vmem_limit_bytes=30 * 1024 * 1024),
        cost_estimate=pl.CostEstimate(
            flops=4 * total * steps * BLOCK * width, bytes_accessed=4 * steps * BLOCK * width, transcendentals=0
        ),
        name="base",
    )(*x_parts, gate_matrix, up_matrix, *sums)


def finish_kernel(gate_ref, up_ref, pick_ref, order_ref, *refs):
    stacked = jnp.concatenate([ref[...] for ref in refs[:-1]], axis=0)
    gate = gate_ref[...] + jnp.dot(pick_ref[...], stacked, preferred_element_type=F32)
    hidden = (gate / (1.0 + jnp.exp(-gate)) * up_ref[...]).astype(BF16)
    refs[-1][...] = jnp.dot(order_ref[...], hidden, preferred_element_type=F32).astype(BF16)


def finish(gate, up, pick, order, rows_by_plane):
    total, width = gate.shape
    step = width // 2 if width % (2 * LANES) == 0 else width
    col = lambda a: pl.BlockSpec((a.shape[0], step), lambda i: (0, i))
    whole = lambda a: pl.BlockSpec(a.shape, lambda i: (0, 0))
    return pl.pallas_call(
        finish_kernel,
        out_shape=jax.ShapeDtypeStruct((total, width), BF16),
        grid=(width // step,),
        in_specs=[col(gate), col(up), whole(pick), whole(order)] + [col(r) for r in rows_by_plane],
        out_specs=pl.BlockSpec((total, step), lambda i: (0, i)),
        compiler_params=pltpu.CompilerParams(vmem_limit_bytes=32 * 1024 * 1024),
        cost_estimate=pl.CostEstimate(flops=0, bytes_accessed=4 * total * width * 4, transcendentals=total * width),
        name="finish",
    )(gate, up, pick, order, *rows_by_plane)


def plane_shards(
    tokens,
    token_adapter_index,
    adapter_slot_index,
    gate_matrix,
    up_matrix,
    adapter_down_factor,
    adapter_up_factor,
):
    count = lax.axis_size("dp")
    me, y = lax.axis_index("dp"), lax.axis_index("groups")
    z = me // 4
    own_rows, depth = tokens.shape
    total = own_rows * count
    width = gate_matrix.shape[1]
    rank = adapter_up_factor.shape[1]

    def swap(value, k):
        return lax.ppermute(value, "dp", [(d, d ^ k) for d in range(count)])

    def other(value):
        return lax.ppermute(value, "groups", [(0, 1), (1, 0)])

    ids = jnp.broadcast_to(token_adapter_index.astype(BF16), (own_rows, LANES))
    packed = jnp.concatenate([tokens, ids], axis=1)
    second, third = swap(packed, 8), swap(packed, 12)
    cross, both = cut_cross(adapter_up_factor[0], width)
    cross, both = swap(cross, 2), swap(both, 3)
    pair = jnp.concatenate([packed, swap(packed, 2)], axis=0)
    remote = jnp.concatenate([second, third], axis=0)
    own_chip, own_plane, core_chip, core_plane = repack(adapter_up_factor[0], width)
    core_chip, core_plane = swap(core_chip, 1), swap(core_plane, 1)
    pair, remote, down, core_chip, core_plane = lax.optimization_barrier(
        (pair, remote, adapter_down_factor[0], core_chip, core_plane)
    )
    close = jnp.concatenate([pair, swap(pair, 4)], axis=0)
    remote = jnp.concatenate([remote, swap(remote, 2)], axis=0)
    close, cross, both = lax.optimization_barrier((close, cross, both))
    x_parts = (close, remote, swap(close, 1), swap(remote, 1))
    distances = [0, 2, 4, 6, 8, 12, 10, 14]
    distances = distances + [k + 1 for k in distances]

    crossed = jnp.concatenate([cross, both], axis=0)
    cross_parts = (crossed, other(crossed))
    half = rank // 2

    place = jnp.arange(total, dtype=jnp.int32)
    order_of = (jnp.repeat(jnp.array(distances, jnp.int32), own_rows) ^ me) * own_rows + place % own_rows
    table = jnp.pad(adapter_slot_index, (0, LANES - count))[None, :]
    low, meta, first, order, rounds = low_rows(x_parts, down.T, table, order_of)
    slots, ranks = meta[0], meta[1]

    def turned(v):
        return jnp.where(y == 0, v, jnp.concatenate([v[:, half:], v[:, :half]], axis=1))

    chip_plan = tuple(((0, i, 0, rank), (1, i, 0, rank)) for i in range(2 * len(ROWS)))
    plane_plan = tuple(
        ((0, i, 0, rank), (1, i, 0, rank)) + tuple((n, i, at, half) for at in (0, half) for n in (2, 3))
        for i in range(len(FACTORS))
    )

    def chip_rows(e):
        return delta_rows(e, (own_chip, core_chip), chip_plan, width)

    def plane_rows(e):
        return delta_rows(e, (own_plane, core_plane, *cross_parts), plane_plan, width)

    def arrived(chip, plane):
        here, first, here_cross, first_cross = chip
        second, third = plane
        return [here, swap(first, 4), swap(second, 8), swap(third, 12), swap(here_cross, 2), swap(first_cross, 6)]

    cross_low, both_low = swap(low, 2), swap(low, 3)
    chip = jnp.concatenate([low, swap(low, 1)], axis=1)
    by_chip = chip_rows(chip[: ROOMS[0]])
    by_chip, cross_low, both_low = lax.optimization_barrier((by_chip, cross_low, both_low))
    plane = jnp.concatenate([chip, turned(cross_low), turned(both_low)], axis=1)
    by_plane = plane_rows(plane[: ROOMS[0]])
    by_plane, x_parts, slots, ranks = lax.optimization_barrier((by_plane, x_parts, slots, ranks))
    rows = arrived(by_chip, by_plane)
    gate, up = base(x_parts, gate_matrix, up_matrix, 0, depth // BLOCK)

    def picked(start, room):
        at = jnp.where((ranks >= start) & (ranks < start + room), ((slots // 4) ^ z) * room + ranks - start, -1)
        pick = (at[:, None] == jnp.arange(PLANES * room, dtype=jnp.int32)[None, :]).astype(BF16)
        return jnp.concatenate([pick, pick[:, : len(ROWS) * room]], axis=1)

    def short():
        return finish(gate, up, first, order, rows)

    def more(room):
        at = slice(ROOMS[0], ROOMS[0] + room)
        rest = arrived(chip_rows(chip[at]), plane_rows(plane[at]))
        pick = jnp.concatenate([first, picked(ROOMS[0], room)], axis=1)
        return finish(gate, up, pick, order, rows + rest)

    return lax.switch(rounds[0], (short, lambda: more(ROOMS[1]), lambda: more(ROOMS[1] + ROOMS[2])))


def solution(mesh):
    in_specs = (
        P(("groups", "dp"), None),
        P(("groups", "dp"), None),
        P(),
        P(None, "dp"),
        P(None, "dp"),
        P("dp", None, None),
        P("dp", None, None),
    )
    out_specs = P("groups", "dp")
    shards = plane_shards if mesh.shape["dp"] == 16 and mesh.shape["groups"] == 2 else general_shards
    return jax.shard_map(shards, mesh=mesh, in_specs=in_specs, out_specs=out_specs, check_vma=False)
```

```python
import functools

import jax
import jax.numpy as jnp
from jax import lax
from jax.experimental import pallas as pl
from jax.experimental.pallas import tpu as pltpu
from jax.sharding import PartitionSpec as P

CAP = 32
LANES = 128
PLANES = 4
F32 = jnp.float32
BF16 = jnp.bfloat16


def general_shards(
    tokens,
    token_adapter_index,
    adapter_slot_index,
    gate_matrix,
    up_matrix,
    adapter_down_factor,
    adapter_up_factor,
):
    count = lax.axis_size("dp")
    myself = lax.axis_index("dp")
    all_rows, all_ids = (
        lax.all_gather(tokens, "dp", axis=0, tiled=True),
        lax.all_gather(token_adapter_index, "dp", axis=0, tiled=True),
    )
    total = all_rows.shape[0]
    places = jnp.arange(count, dtype=jnp.int32)
    match = all_ids[:, 0][:, None] == places[None, :]
    slots = jnp.sum(jnp.where(match, adapter_slot_index[None, :], 0), 1)
    slot_match = slots[:, None] == places[None, :]
    onehot = slot_match.astype(jnp.int32)
    ranks = jnp.sum(jnp.cumsum(onehot, 0) * onehot, 1) - 1
    capacity = CAP
    columns = jnp.arange(capacity, dtype=jnp.int32)
    mine = (slots == myself)[:, None] & (ranks[:, None] == columns[None, :])
    row_list = jnp.sum(jnp.where(mine, jnp.arange(total, dtype=jnp.int32)[:, None], 0), 0)
    selected_slot = jnp.take(all_rows, row_list, axis=0)
    reduced_rows = jnp.dot(
        selected_slot, adapter_down_factor[0], preferred_element_type=F32
    ).astype(BF16)
    slot_pieces = lax.all_to_all(adapter_up_factor, "dp", split_axis=2, concat_axis=0, tiled=True)
    all_low = lax.all_gather(reduced_rows, "dp", axis=0, tiled=True)
    rank_width = all_low.shape[1]
    token_low = jnp.take(all_low, slots * capacity + ranks, axis=0)
    expanded = (token_low[:, None, :] * slot_match.astype(BF16)[:, :, None]).reshape(
        total, count * rank_width
    )
    stacked = slot_pieces.reshape(count * rank_width, slot_pieces.shape[2])
    delta = jnp.dot(expanded, stacked, preferred_element_type=F32).astype(BF16)
    gate_base = jnp.dot(all_rows, gate_matrix, preferred_element_type=F32)
    up = jnp.dot(all_rows, up_matrix, preferred_element_type=F32)
    gate = gate_base + delta.astype(F32)
    return (jax.nn.silu(gate) * up).astype(BF16)


ANY = pl.BlockSpec(memory_space=pl.ANY)
HBM = pl.BlockSpec(memory_space=pltpu.HBM)
VMEM = pl.BlockSpec(memory_space=pltpu.VMEM)
ROOMS = (64, 16, 48)
FACTORS = (2, 3)
ROWS = (0, 1)


def cut(u_ref, held, in_sems, out_sems, width, wanted):
    rank = u_ref.shape[0]
    half = rank // 2
    z = lax.axis_index("dp") // 4
    ins, sends = [], []
    for n, (j, x, c, part, target) in enumerate(wanted):
        at = pl.multiple_of(((lax.bitwise_xor(z, j) * 2 + x) * 2 + c) * width, LANES)
        rows = pl.ds(0, rank) if part is None else pl.ds(pl.multiple_of(part * half, half), half)
        here = held.at[pl.ds(0, rank if part is None else half), pl.ds(n * width, width)]
        ins.append(pltpu.make_async_copy(u_ref.at[rows, pl.ds(at, width)], here, in_sems.at[n]))
        sends.append(pltpu.make_async_copy(here, target, out_sems.at[n]))
    for copy in ins:
        copy.start()
    for copy, send in zip(ins, sends):
        copy.wait()
        send.start()
    for send in sends:
        send.wait()


def position():
    me = lax.axis_index("dp")
    return (me // 2) % 2, me % 2


def cross_kernel(width, u_ref, cross_ref, both_ref, *scratch):
    (x, c), y = position(), lax.axis_index("groups")
    wanted = []
    for i, j in enumerate(FACTORS):
        place = pl.ds(i * width, width)
        wanted += [(j, 1 - x, c, y, cross_ref.at[:, place]), (j, 1 - x, 1 - c, y, both_ref.at[:, place])]
    cut(u_ref, *scratch, width, wanted)


def cut_cross(u, width):
    rank = u.shape[0]
    n = 2 * len(FACTORS)
    split = jax.ShapeDtypeStruct((rank // 2, len(FACTORS) * width), BF16)
    return pl.pallas_call(
        functools.partial(cross_kernel, width),
        out_shape=[split, split],
        in_specs=[HBM],
        out_specs=[ANY, ANY],
        scratch_shapes=[
            pltpu.VMEM((rank // 2, n * width), BF16),
            pltpu.SemaphoreType.DMA((n,)),
            pltpu.SemaphoreType.DMA((n,)),
        ],
        compiler_params=pltpu.CompilerParams(vmem_limit_bytes=61 * 1024 * 1024),
        cost_estimate=pl.CostEstimate(flops=0, bytes_accessed=2 * rank * n * width, transcendentals=0),
        name="cut_cross",
    )(u)


def repack_kernel(width, u_ref, own_rows_ref, own_ref, core_rows_ref, core_ref, *scratch):
    x, c = position()
    wanted = []
    for cc, rows_ref, ref in ((1 - c, core_rows_ref, core_ref), (c, own_rows_ref, own_ref)):
        for target, blocks in (
            (ref, [(j, x) for j in FACTORS]),
            (rows_ref, [(j, xx) for xx in (x, 1 - x) for j in ROWS]),
        ):
            for i, (j, xx) in enumerate(blocks):
                wanted.append((j, xx, cc, None, target.at[:, pl.ds(i * width, width)]))
    cut(u_ref, *scratch, width, wanted)


def repack(u, width):
    rank = u.shape[0]
    n = 2 * (len(FACTORS) + 2 * len(ROWS))
    for_rows = jax.ShapeDtypeStruct((rank, 2 * len(ROWS) * width), BF16)
    for_factors = jax.ShapeDtypeStruct((rank, len(FACTORS) * width), BF16)
    return pl.pallas_call(
        functools.partial(repack_kernel, width),
        out_shape=[for_rows, for_factors] * 2,
        in_specs=[HBM],
        out_specs=[ANY] * 4,
        scratch_shapes=[
            pltpu.VMEM((rank, n * width), BF16),
            pltpu.SemaphoreType.DMA((n,)),
            pltpu.SemaphoreType.DMA((n,)),
        ],
        compiler_params=pltpu.CompilerParams(vmem_limit_bytes=61 * 1024 * 1024),
        cost_estimate=pl.CostEstimate(flops=0, bytes_accessed=3 * u.size, transcendentals=0),
        name="repack",
    )(u)


def low_kernel(*refs):
    x_refs, (down_ref, table_ref, at_ref, at_column_ref), outs = refs[:4], refs[4:8], refs[8:]
    low_ref, meta_ref, pick_ref, order_ref, rounds_ref = outs
    depth = down_ref.shape[1]
    x = jnp.concatenate([ref[:, :depth] for ref in x_refs], axis=0)
    low = lax.dot_general(x, down_ref[...], (((1,), (1,)), ((), ())), preferred_element_type=F32).astype(BF16)
    ids = jnp.concatenate([ref[:, depth:] for ref in x_refs], axis=0).astype(F32)
    total = ids.shape[0]
    lane = lax.broadcasted_iota(jnp.int32, ids.shape, 1).astype(F32)
    place = lax.broadcasted_iota(jnp.int32, ids.shape, 0).astype(F32)
    table = jnp.broadcast_to(table_ref[...], ids.shape).astype(F32)
    slots = jnp.broadcast_to(jnp.sum(jnp.where(ids == lane, table, 0.0), axis=1, keepdims=True), (total, total))
    slots_row = slots.T
    planes, planes_row = jnp.floor(slots * 0.25), jnp.floor(slots_row * 0.25)
    at = jnp.broadcast_to(at_ref[...], ids.shape).astype(F32)
    at_column = jnp.broadcast_to(at_column_ref[...], ids.shape).astype(F32)
    same = planes == planes_row
    ranks_row = jnp.sum(jnp.where(same & (at_column < at), 1.0, 0.0), axis=0, keepdims=True)
    ranks = jnp.sum(jnp.where(same & (at < at_column), 1.0, 0.0), axis=1, keepdims=True)
    me = lax.axis_index("dp")
    mine = jnp.where((slots_row == me.astype(F32)) & (ranks_row == place), 1.0, 0.0).astype(BF16)
    low_ref[...] = jnp.dot(mine, low, preferred_element_type=F32).astype(BF16)
    meta_ref[0:1, :] = slots_row[0:1, :].astype(jnp.int32)
    meta_ref[1:2, :] = ranks_row.astype(jnp.int32)
    order_ref[...] = jnp.where(at == place, 1.0, 0.0).astype(BF16)
    room = ROOMS[0]
    wide = lax.broadcasted_iota(jnp.int32, pick_ref.shape, 1)
    block = wide // room
    distance = jnp.where(block < PLANES, block, block - PLANES)
    wanted = lax.bitwise_xor(distance, jnp.broadcast_to(me // 4, distance.shape)).astype(F32)
    found = (planes[:, :1] == wanted) & (ranks == (wide % room).astype(F32))
    pick_ref[...] = jnp.where(found, 1.0, 0.0).astype(BF16)
    most = jnp.max(ranks_row)
    rounds_ref[0] = (most >= room).astype(jnp.int32) + (most >= room + ROOMS[1]).astype(jnp.int32)


def low_rows(x_parts, down, table, order_of):
    total = order_of.shape[0]
    rank = down.shape[0]
    return pl.pallas_call(
        low_kernel,
        out_shape=[
            jax.ShapeDtypeStruct((total, rank), BF16),
            jax.ShapeDtypeStruct((2, total), jnp.int32),
            jax.ShapeDtypeStruct((total, (PLANES + len(ROWS)) * ROOMS[0]), BF16),
            jax.ShapeDtypeStruct((total, total), BF16),
            jax.ShapeDtypeStruct((1,), jnp.int32),
        ],
        in_specs=[VMEM] * 8,
        out_specs=[VMEM] * 4 + [pl.BlockSpec(memory_space=pltpu.SMEM)],
        compiler_params=pltpu.CompilerParams(vmem_limit_bytes=16 * 1024 * 1024),
        cost_estimate=pl.CostEstimate(flops=0, bytes_accessed=4096, transcendentals=0),
        name="low_rows",
    )(*x_parts, down, table, order_of[None, :], order_of[:, None])


def delta_kernel(plan, width, e_ref, *refs):
    parts, outs = refs[: len(refs) - len(plan)], refs[len(refs) - len(plan) :]
    for pieces, out in zip(plan, outs):
        stacked = jnp.concatenate(
            [parts[n][at : at + rows, i * width : (i + 1) * width] for n, i, at, rows in pieces], axis=0
        )
        out[...] = jnp.dot(e_ref[:, : stacked.shape[0]], stacked, preferred_element_type=F32).astype(BF16)


def delta_rows(e, parts, plan, width):
    rows = e.shape[0]
    n = len(plan)
    return pl.pallas_call(
        functools.partial(delta_kernel, plan, width),
        out_shape=[jax.ShapeDtypeStruct((rows, width), BF16)] * n,
        in_specs=[VMEM] * (1 + len(parts)),
        out_specs=[VMEM] * n,
        compiler_params=pltpu.CompilerParams(vmem_limit_bytes=8 * 1024 * 1024),
        cost_estimate=pl.CostEstimate(flops=0, bytes_accessed=4096, transcendentals=0),
        name="delta_rows",
    )(e, *parts)


BLOCK = 512
SLOTS = 3
AHEAD = 4


def fetch_kernel(first, after_ref, ref, head_ref, sem):
    copy = pltpu.make_async_copy(ref.at[pl.ds(first, head_ref.shape[0])], head_ref, sem)
    copy.start()
    copy.wait()


def fetch(after, matrix):
    shape = jax.ShapeDtypeStruct((AHEAD * BLOCK, matrix.shape[1]), BF16)
    return pl.pallas_call(
        functools.partial(fetch_kernel, 0),
        out_shape=shape,
        in_specs=[ANY, HBM],
        out_specs=VMEM,
        scratch_shapes=[pltpu.SemaphoreType.DMA],
        compiler_params=pltpu.CompilerParams(vmem_limit_bytes=24 * 1024 * 1024),
        cost_estimate=pl.CostEstimate(flops=0, bytes_accessed=8 * shape.size, transcendentals=0),
        name="fetch",
    )(after, matrix)


def base_kernel(steps, rows, *refs):
    x_refs, (g_ref, u_ref, g_head, u_head), refs = refs[:4], refs[4:8], refs[8:]
    gate_ref, up_ref, x_held, g_held, u_held, x_sems, g_sems, u_sems = refs

    def weights(k, slot):
        at = pl.ds(pl.multiple_of(k * BLOCK, BLOCK), BLOCK)
        return (
            pltpu.make_async_copy(g_ref.at[at], g_held.at[slot], g_sems.at[slot]),
            pltpu.make_async_copy(u_ref.at[at], u_held.at[slot], u_sems.at[slot]),
        )

    columns = pl.ds(0, steps * BLOCK)
    loads = [
        pltpu.make_async_copy(ref.at[:, columns], x_held.at[pl.ds(i * rows, rows)], x_sems.at[i])
        for i, ref in enumerate(x_refs)
    ]
    for copy in loads:
        copy.start()
    for k in range(SLOTS):
        for copy in weights(AHEAD + k, k):
            copy.start()
    for copy in loads:
        copy.wait()
    x = x_held[:, : AHEAD * BLOCK]
    gate_ref[...] = jnp.dot(x, g_head[...], preferred_element_type=F32)
    up_ref[...] = jnp.dot(x, u_head[...], preferred_element_type=F32)

    def step(n, carry):
        slot = lax.rem(n, SLOTS)
        k = n + AHEAD
        gate_copy, up_copy = weights(k, slot)
        x = x_held[:, pl.ds(pl.multiple_of(k * BLOCK, BLOCK), BLOCK)]
        gate_copy.wait()
        gate_ref[...] += jnp.dot(x, g_held[slot], preferred_element_type=F32)
        up_copy.wait()
        up_ref[...] += jnp.dot(x, u_held[slot], preferred_element_type=F32)

        @pl.when(k + SLOTS < steps)
        def _():
            for copy in weights(k + SLOTS, slot):
                copy.start()

        return carry

    lax.fori_loop(0, steps - AHEAD, step, 0)


def base(x_parts, gate_matrix, up_matrix, heads):
    depth, width = gate_matrix.shape
    steps = depth // BLOCK
    rows = x_parts[0].shape[0]
    total = rows * len(x_parts)
    shape = jax.ShapeDtypeStruct((total, width), F32)
    return pl.pallas_call(
        functools.partial(base_kernel, steps, rows),
        out_shape=[shape, shape],
        in_specs=[ANY] * len(x_parts) + [HBM] * 2 + [VMEM] * 2,
        out_specs=[VMEM, VMEM],
        scratch_shapes=[
            pltpu.VMEM((total, depth), BF16),
            pltpu.VMEM((SLOTS, BLOCK, width), BF16),
            pltpu.VMEM((SLOTS, BLOCK, width), BF16),
            pltpu.SemaphoreType.DMA((len(x_parts),)),
            pltpu.SemaphoreType.DMA((SLOTS,)),
            pltpu.SemaphoreType.DMA((SLOTS,)),
        ],
        compiler_params=pltpu.CompilerParams(vmem_limit_bytes=36 * 1024 * 1024),
        cost_estimate=pl.CostEstimate(
            flops=4 * total * depth * width, bytes_accessed=4 * depth * width, transcendentals=0
        ),
        name="base",
    )(*x_parts, gate_matrix, up_matrix, *heads)


def finish_kernel(gate_ref, up_ref, pick_ref, order_ref, *refs):
    stacked = jnp.concatenate([ref[...] for ref in refs[:-1]], axis=0)
    gate = gate_ref[...] + jnp.dot(pick_ref[...], stacked, preferred_element_type=F32)
    hidden = (gate / (1.0 + jnp.exp(-gate)) * up_ref[...]).astype(BF16)
    refs[-1][...] = jnp.dot(order_ref[...], hidden, preferred_element_type=F32).astype(BF16)


def finish(gate, up, pick, order, rows_by_plane):
    total, width = gate.shape
    step = width // 2 if width % (2 * LANES) == 0 else width
    col = lambda a: pl.BlockSpec((a.shape[0], step), lambda i: (0, i))
    whole = lambda a: pl.BlockSpec(a.shape, lambda i: (0, 0))
    return pl.pallas_call(
        finish_kernel,
        out_shape=jax.ShapeDtypeStruct((total, width), BF16),
        grid=(width // step,),
        in_specs=[col(gate), col(up), whole(pick), whole(order)] + [col(r) for r in rows_by_plane],
        out_specs=pl.BlockSpec((total, step), lambda i: (0, i)),
        compiler_params=pltpu.CompilerParams(vmem_limit_bytes=32 * 1024 * 1024),
        cost_estimate=pl.CostEstimate(flops=0, bytes_accessed=4 * total * width * 4, transcendentals=total * width),
        name="finish",
    )(gate, up, pick, order, *rows_by_plane)


def plane_shards(
    tokens,
    token_adapter_index,
    adapter_slot_index,
    gate_matrix,
    up_matrix,
    adapter_down_factor,
    adapter_up_factor,
):
    count = lax.axis_size("dp")
    me, y = lax.axis_index("dp"), lax.axis_index("groups")
    z = me // 4
    own_rows, depth = tokens.shape
    total = own_rows * count
    width = gate_matrix.shape[1]
    rank = adapter_up_factor.shape[1]

    def swap(value, k):
        return lax.ppermute(value, "dp", [(d, d ^ k) for d in range(count)])

    def other(value):
        return lax.ppermute(value, "groups", [(0, 1), (1, 0)])

    ids = jnp.broadcast_to(token_adapter_index.astype(BF16), (own_rows, LANES))
    packed = jnp.concatenate([tokens, ids], axis=1)
    second, third = swap(packed, 8), swap(packed, 12)
    cross, both = cut_cross(adapter_up_factor[0], width)
    cross, both = swap(cross, 2), swap(both, 3)
    pair = jnp.concatenate([packed, swap(packed, 2)], axis=0)
    remote = jnp.concatenate([second, third], axis=0)
    own_chip, own_plane, core_chip, core_plane = repack(adapter_up_factor[0], width)
    core_chip, core_plane = swap(core_chip, 1), swap(core_plane, 1)
    pair, remote, down, core_chip, core_plane = lax.optimization_barrier(
        (pair, remote, adapter_down_factor[0], core_chip, core_plane)
    )
    close = jnp.concatenate([pair, swap(pair, 4)], axis=0)
    remote = jnp.concatenate([remote, swap(remote, 2)], axis=0)
    gate_head = fetch(pair, gate_matrix)
    cross, both, gate_head = lax.optimization_barrier((cross, both, gate_head))
    crossed = jnp.concatenate([cross, both], axis=0)
    up_head = fetch(crossed, up_matrix)
    heads = (gate_head, up_head)
    close, remote, heads = lax.optimization_barrier((close, remote, heads))
    x_parts = (close, remote, swap(close, 1), swap(remote, 1))
    distances = [0, 2, 4, 6, 8, 12, 10, 14]
    distances = distances + [k + 1 for k in distances]

    cross_parts = (crossed, other(crossed))
    half = rank // 2

    place = jnp.arange(total, dtype=jnp.int32)
    order_of = (jnp.repeat(jnp.array(distances, jnp.int32), own_rows) ^ me) * own_rows + place % own_rows
    table = jnp.pad(adapter_slot_index, (0, LANES - count))[None, :]
    low, meta, first, order, rounds = low_rows(x_parts, down.T, table, order_of)
    slots, ranks = meta[0], meta[1]

    def turned(v):
        return jnp.where(y == 0, v, jnp.concatenate([v[:, half:], v[:, :half]], axis=1))

    chip_plan = tuple(((0, i, 0, rank), (1, i, 0, rank)) for i in range(2 * len(ROWS)))
    plane_plan = tuple(
        ((0, i, 0, rank), (1, i, 0, rank)) + tuple((n, i, at, half) for at in (0, half) for n in (2, 3))
        for i in range(len(FACTORS))
    )

    def chip_rows(e):
        return delta_rows(e, (own_chip, core_chip), chip_plan, width)

    def plane_rows(e):
        return delta_rows(e, (own_plane, core_plane, *cross_parts), plane_plan, width)

    def arrived(chip, plane):
        here, first, here_cross, first_cross = chip
        second, third = plane
        return [here, swap(first, 4), swap(second, 8), swap(third, 12), swap(here_cross, 2), swap(first_cross, 6)]

    cross_low, both_low = swap(low, 2), swap(low, 3)
    chip = jnp.concatenate([low, swap(low, 1)], axis=1)
    by_chip = chip_rows(chip[: ROOMS[0]])
    by_chip, cross_low, both_low = lax.optimization_barrier((by_chip, cross_low, both_low))
    plane = jnp.concatenate([chip, turned(cross_low), turned(both_low)], axis=1)
    by_plane = plane_rows(plane[: ROOMS[0]])
    by_plane, x_parts, slots, ranks = lax.optimization_barrier((by_plane, x_parts, slots, ranks))
    rows = arrived(by_chip, by_plane)
    gate, up = base(x_parts, gate_matrix, up_matrix, heads)

    def picked(start, room):
        at = jnp.where((ranks >= start) & (ranks < start + room), ((slots // 4) ^ z) * room + ranks - start, -1)
        pick = (at[:, None] == jnp.arange(PLANES * room, dtype=jnp.int32)[None, :]).astype(BF16)
        return jnp.concatenate([pick, pick[:, : len(ROWS) * room]], axis=1)

    def short():
        return finish(gate, up, first, order, rows)

    def more(room):
        at = slice(ROOMS[0], ROOMS[0] + room)
        rest = arrived(chip_rows(chip[at]), plane_rows(plane[at]))
        pick = jnp.concatenate([first, picked(ROOMS[0], room)], axis=1)
        return finish(gate, up, pick, order, rows + rest)

    return lax.switch(rounds[0], (short, lambda: more(ROOMS[1]), lambda: more(ROOMS[1] + ROOMS[2])))


def solution(mesh):
    in_specs = (
        P(("groups", "dp"), None),
        P(("groups", "dp"), None),
        P(),
        P(None, "dp"),
        P(None, "dp"),
        P("dp", None, None),
        P("dp", None, None),
    )
    out_specs = P("groups", "dp")
    shards = plane_shards if mesh.shape["dp"] == 16 and mesh.shape["groups"] == 2 else general_shards
    return jax.shard_map(shards, mesh=mesh, in_specs=in_specs, out_specs=out_specs, check_vma=False)
```

```python
import functools

import jax
import jax.numpy as jnp
from jax import lax
from jax.experimental import pallas as pl
from jax.experimental.pallas import tpu as pltpu
from jax.sharding import PartitionSpec as P

CAP = 32
LANES = 128
PLANES = 4
F32 = jnp.float32
BF16 = jnp.bfloat16


def general_shards(
    tokens,
    token_adapter_index,
    adapter_slot_index,
    gate_matrix,
    up_matrix,
    adapter_down_factor,
    adapter_up_factor,
):
    count = lax.axis_size("dp")
    myself = lax.axis_index("dp")
    all_rows, all_ids = (
        lax.all_gather(tokens, "dp", axis=0, tiled=True),
        lax.all_gather(token_adapter_index, "dp", axis=0, tiled=True),
    )
    total = all_rows.shape[0]
    places = jnp.arange(count, dtype=jnp.int32)
    match = all_ids[:, 0][:, None] == places[None, :]
    slots = jnp.sum(jnp.where(match, adapter_slot_index[None, :], 0), 1)
    slot_match = slots[:, None] == places[None, :]
    onehot = slot_match.astype(jnp.int32)
    ranks = jnp.sum(jnp.cumsum(onehot, 0) * onehot, 1) - 1
    capacity = CAP
    columns = jnp.arange(capacity, dtype=jnp.int32)
    mine = (slots == myself)[:, None] & (ranks[:, None] == columns[None, :])
    row_list = jnp.sum(jnp.where(mine, jnp.arange(total, dtype=jnp.int32)[:, None], 0), 0)
    selected_slot = jnp.take(all_rows, row_list, axis=0)
    reduced_rows = jnp.dot(
        selected_slot, adapter_down_factor[0], preferred_element_type=F32
    ).astype(BF16)
    slot_pieces = lax.all_to_all(adapter_up_factor, "dp", split_axis=2, concat_axis=0, tiled=True)
    all_low = lax.all_gather(reduced_rows, "dp", axis=0, tiled=True)
    rank_width = all_low.shape[1]
    token_low = jnp.take(all_low, slots * capacity + ranks, axis=0)
    expanded = (token_low[:, None, :] * slot_match.astype(BF16)[:, :, None]).reshape(
        total, count * rank_width
    )
    stacked = slot_pieces.reshape(count * rank_width, slot_pieces.shape[2])
    delta = jnp.dot(expanded, stacked, preferred_element_type=F32).astype(BF16)
    gate_base = jnp.dot(all_rows, gate_matrix, preferred_element_type=F32)
    up = jnp.dot(all_rows, up_matrix, preferred_element_type=F32)
    gate = gate_base + delta.astype(F32)
    return (jax.nn.silu(gate) * up).astype(BF16)


ANY = pl.BlockSpec(memory_space=pl.ANY)
HBM = pl.BlockSpec(memory_space=pltpu.HBM)
VMEM = pl.BlockSpec(memory_space=pltpu.VMEM)
ROOMS = (64, 16, 48)
FACTORS = (2, 3)
ROWS = (0, 1)


def cut(u_ref, sems, width, wanted):
    rank = u_ref.shape[0]
    half = rank // 2
    z = lax.axis_index("dp") // 4
    copies = []
    for n, (j, x, c, part, target) in enumerate(wanted):
        at = pl.multiple_of(((lax.bitwise_xor(z, j) * 2 + x) * 2 + c) * width, LANES)
        rows = pl.ds(0, rank) if part is None else pl.ds(pl.multiple_of(part * half, half), half)
        copies.append(pltpu.make_async_copy(u_ref.at[rows, pl.ds(at, width)], target, sems.at[n]))
    for copy in copies:
        copy.start()
    for copy in copies:
        copy.wait()


def position():
    me = lax.axis_index("dp")
    return (me // 2) % 2, me % 2


def cross_kernel(width, u_ref, cross_ref, both_ref, sems):
    (x, c), y = position(), lax.axis_index("groups")
    wanted = []
    for i, j in enumerate(FACTORS):
        place = pl.ds(i * width, width)
        wanted += [(j, 1 - x, c, y, cross_ref.at[:, place]), (j, 1 - x, 1 - c, y, both_ref.at[:, place])]
    cut(u_ref, sems, width, wanted)


def cut_cross(u, width):
    rank = u.shape[0]
    n = 2 * len(FACTORS)
    split = pltpu.VMEM((rank // 2, len(FACTORS) * width), BF16)
    return pl.pallas_call(
        functools.partial(cross_kernel, width),
        out_shape=[split, split],
        in_specs=[HBM],
        out_specs=[VMEM, VMEM],
        scratch_shapes=[pltpu.SemaphoreType.DMA((n,))],
        compiler_params=pltpu.CompilerParams(vmem_limit_bytes=4 * 1024 * 1024),
        cost_estimate=pl.CostEstimate(flops=0, bytes_accessed=2 * rank * n * width, transcendentals=0),
        name="cut_cross",
    )(u)


def repack_kernel(width, u_ref, own_rows_ref, own_ref, core_rows_ref, core_ref, sems):
    x, c = position()
    wanted = []
    for cc, rows_ref, ref in ((1 - c, core_rows_ref, core_ref), (c, own_rows_ref, own_ref)):
        for target, blocks in (
            (ref, [(j, x) for j in FACTORS]),
            (rows_ref, [(j, xx) for xx in (x, 1 - x) for j in ROWS]),
        ):
            for i, (j, xx) in enumerate(blocks):
                wanted.append((j, xx, cc, None, target.at[:, pl.ds(i * width, width)]))
    cut(u_ref, sems, width, wanted)


def repack(u, width):
    rank = u.shape[0]
    n = 2 * (len(FACTORS) + 2 * len(ROWS))
    for_rows = pltpu.VMEM((rank, 2 * len(ROWS) * width), BF16)
    for_factors = pltpu.VMEM((rank, len(FACTORS) * width), BF16)
    return pl.pallas_call(
        functools.partial(repack_kernel, width),
        out_shape=[for_rows, for_factors] * 2,
        in_specs=[HBM],
        out_specs=[VMEM] * 4,
        scratch_shapes=[pltpu.SemaphoreType.DMA((n,))],
        compiler_params=pltpu.CompilerParams(vmem_limit_bytes=4 * 1024 * 1024),
        cost_estimate=pl.CostEstimate(flops=0, bytes_accessed=3 * u.size, transcendentals=0),
        name="repack",
    )(u)


def low_kernel(*refs):
    x_refs, (down_ref, table_ref, distance_ref, distance_column_ref), outs = refs[:4], refs[4:8], refs[8:]
    low_ref, meta_ref, pick_ref, order_ref, rounds_ref = outs
    depth = down_ref.shape[1]
    x = jnp.concatenate([ref[:, :depth] for ref in x_refs], axis=0)
    low = lax.dot_general(x, down_ref[...], (((1,), (1,)), ((), ())), preferred_element_type=F32).astype(BF16)
    ids = jnp.concatenate([ref[:, depth:] for ref in x_refs], axis=0).astype(F32)
    total = ids.shape[0]
    lane = lax.broadcasted_iota(jnp.int32, ids.shape, 1).astype(F32)
    place = lax.broadcasted_iota(jnp.int32, ids.shape, 0).astype(F32)
    table = jnp.broadcast_to(table_ref[...], ids.shape).astype(F32)
    slots = jnp.broadcast_to(jnp.sum(jnp.where(ids == lane, table, 0.0), axis=1, keepdims=True), (total, total))
    slots_row = slots.T
    planes, planes_row = jnp.floor(slots * 0.25), jnp.floor(slots_row * 0.25)
    me = lax.axis_index("dp")
    own_rows = total // lax.axis_size("dp")

    def rows_at(distance, along):
        inner = lax.broadcasted_iota(jnp.int32, ids.shape, along) % own_rows
        owner = lax.bitwise_xor(jnp.broadcast_to(distance, ids.shape), jnp.broadcast_to(me, ids.shape))
        return (owner * own_rows + inner).astype(F32)

    at, at_column = rows_at(distance_ref[...], 1), rows_at(distance_column_ref[...], 0)
    same = planes == planes_row
    ranks_row = jnp.sum(jnp.where(same & (at_column < at), 1.0, 0.0), axis=0, keepdims=True)
    ranks = jnp.sum(jnp.where(same & (at < at_column), 1.0, 0.0), axis=1, keepdims=True)
    mine = jnp.where((slots_row == me.astype(F32)) & (ranks_row == place), 1.0, 0.0).astype(BF16)
    low_ref[...] = jnp.dot(mine, low, preferred_element_type=F32).astype(BF16)
    z = jnp.broadcast_to(me // 4, (1, total))
    meta_ref[0:1, :] = lax.bitwise_xor(planes_row[0:1, :].astype(jnp.int32), z)
    meta_ref[1:2, :] = ranks_row.astype(jnp.int32)
    order_ref[...] = jnp.where(at == place, 1.0, 0.0).astype(BF16)
    room = ROOMS[0]
    wide = lax.broadcasted_iota(jnp.int32, pick_ref.shape, 1)
    block = wide // room
    distance = jnp.where(block < PLANES, block, block - PLANES)
    wanted = lax.bitwise_xor(distance, jnp.broadcast_to(me // 4, distance.shape)).astype(F32)
    found = (planes[:, :1] == wanted) & (ranks == (wide % room).astype(F32))
    pick_ref[...] = jnp.where(found, 1.0, 0.0).astype(BF16)
    most = jnp.max(ranks_row)
    rounds_ref[0] = (most >= room).astype(jnp.int32) + (most >= room + ROOMS[1]).astype(jnp.int32)


def low_rows(x_parts, down, table, distance):
    total = distance.shape[0]
    rank = down.shape[0]
    return pl.pallas_call(
        low_kernel,
        out_shape=[
            jax.ShapeDtypeStruct((total, rank), BF16),
            jax.ShapeDtypeStruct((2, total), jnp.int32),
            jax.ShapeDtypeStruct((total, (PLANES + len(ROWS)) * ROOMS[0]), BF16),
            jax.ShapeDtypeStruct((total, total), BF16),
            jax.ShapeDtypeStruct((1,), jnp.int32),
        ],
        in_specs=[VMEM] * 8,
        out_specs=[VMEM] * 4 + [pl.BlockSpec(memory_space=pltpu.SMEM)],
        compiler_params=pltpu.CompilerParams(vmem_limit_bytes=8 * 1024 * 1024),
        cost_estimate=pl.CostEstimate(flops=0, bytes_accessed=4096, transcendentals=0),
        name="low_rows",
    )(*x_parts, down, table, distance[None, :], distance[:, None])


def delta_kernel(plan, width, e_ref, *refs):
    parts, outs = refs[: len(refs) - len(plan)], refs[len(refs) - len(plan) :]
    e = e_ref[...]
    chip = 2 * parts[0].shape[0]
    if e.shape[1] > chip:
        shape = (e.shape[1] - chip,) * 2
        half = jnp.broadcast_to(lax.axis_index("groups") * (chip // 4), shape)
        here, there = lax.broadcasted_iota(jnp.int32, shape, 0), lax.broadcasted_iota(jnp.int32, shape, 1)
        turn = jnp.where(lax.bitwise_xor(here, half) == there, 1.0, 0.0).astype(BF16)
        beyond = jnp.dot(e[:, chip:], turn, preferred_element_type=F32).astype(BF16)
        e = jnp.concatenate([e[:, :chip], beyond], axis=1)
    for pieces, out in zip(plan, outs):
        stacked = jnp.concatenate(
            [parts[n][at : at + rows, i * width : (i + 1) * width] for n, i, at, rows in pieces], axis=0
        )
        out[...] = jnp.dot(e[:, : stacked.shape[0]], stacked, preferred_element_type=F32).astype(BF16)


def delta_rows(e, parts, plan, width):
    rows = e.shape[0]
    n = len(plan)
    return pl.pallas_call(
        functools.partial(delta_kernel, plan, width),
        out_shape=[jax.ShapeDtypeStruct((rows, width), BF16)] * n,
        in_specs=[VMEM] * (1 + len(parts)),
        out_specs=[VMEM] * n,
        compiler_params=pltpu.CompilerParams(vmem_limit_bytes=8 * 1024 * 1024),
        cost_estimate=pl.CostEstimate(flops=0, bytes_accessed=4096, transcendentals=0),
        name="delta_rows",
    )(e, *parts)


BLOCK = 512
SLOTS = 3
AHEAD = 4


def fetch_kernel(first, after_ref, ref, head_ref, sem):
    copy = pltpu.make_async_copy(ref.at[pl.ds(first, head_ref.shape[0])], head_ref, sem)
    copy.start()
    copy.wait()


def fetch(after, matrix):
    shape = jax.ShapeDtypeStruct((AHEAD * BLOCK, matrix.shape[1]), BF16)
    return pl.pallas_call(
        functools.partial(fetch_kernel, 0),
        out_shape=shape,
        in_specs=[ANY, HBM],
        out_specs=VMEM,
        scratch_shapes=[pltpu.SemaphoreType.DMA],
        compiler_params=pltpu.CompilerParams(vmem_limit_bytes=4 * 1024 * 1024),
        cost_estimate=pl.CostEstimate(flops=0, bytes_accessed=8 * shape.size, transcendentals=0),
        name="fetch",
    )(after, matrix)


def base_kernel(steps, rows, *refs):
    x_refs, (g_ref, u_ref, g_head, u_head), refs = refs[:4], refs[4:8], refs[8:]
    gate_ref, up_ref, x_held, g_held, u_held, x_sems, g_sems, u_sems = refs

    def weights(k, slot):
        at = pl.ds(pl.multiple_of(k * BLOCK, BLOCK), BLOCK)
        return (
            pltpu.make_async_copy(g_ref.at[at], g_held.at[slot], g_sems.at[slot]),
            pltpu.make_async_copy(u_ref.at[at], u_held.at[slot], u_sems.at[slot]),
        )

    columns = pl.ds(0, steps * BLOCK)
    loads = [
        pltpu.make_async_copy(ref.at[:, columns], x_held.at[pl.ds(i * rows, rows)], x_sems.at[i])
        for i, ref in enumerate(x_refs)
    ]
    for copy in loads:
        copy.start()
    for k in range(SLOTS):
        for copy in weights(AHEAD + k, k):
            copy.start()
    for copy in loads:
        copy.wait()
    x = x_held[:, : AHEAD * BLOCK]
    gate_ref[...] = jnp.dot(x, g_head[...], preferred_element_type=F32)
    up_ref[...] = jnp.dot(x, u_head[...], preferred_element_type=F32)

    def step(n, carry):
        slot = lax.rem(n, SLOTS)
        k = n + AHEAD
        gate_copy, up_copy = weights(k, slot)
        x = x_held[:, pl.ds(pl.multiple_of(k * BLOCK, BLOCK), BLOCK)]
        gate_copy.wait()
        gate_ref[...] += jnp.dot(x, g_held[slot], preferred_element_type=F32)
        up_copy.wait()
        up_ref[...] += jnp.dot(x, u_held[slot], preferred_element_type=F32)

        @pl.when(k + SLOTS < steps)
        def _():
            for copy in weights(k + SLOTS, slot):
                copy.start()

        return carry

    lax.fori_loop(0, steps - AHEAD, step, 0)


def base(x_parts, gate_matrix, up_matrix, heads):
    depth, width = gate_matrix.shape
    steps = depth // BLOCK
    rows = x_parts[0].shape[0]
    total = rows * len(x_parts)
    shape = jax.ShapeDtypeStruct((total, width), F32)
    return pl.pallas_call(
        functools.partial(base_kernel, steps, rows),
        out_shape=[shape, shape],
        in_specs=[ANY] * len(x_parts) + [HBM] * 2 + [VMEM] * 2,
        out_specs=[VMEM, VMEM],
        scratch_shapes=[
            pltpu.VMEM((total, depth), BF16),
            pltpu.VMEM((SLOTS, BLOCK, width), BF16),
            pltpu.VMEM((SLOTS, BLOCK, width), BF16),
            pltpu.SemaphoreType.DMA((len(x_parts),)),
            pltpu.SemaphoreType.DMA((SLOTS,)),
            pltpu.SemaphoreType.DMA((SLOTS,)),
        ],
        compiler_params=pltpu.CompilerParams(vmem_limit_bytes=18 * 1024 * 1024),
        cost_estimate=pl.CostEstimate(
            flops=4 * total * depth * width, bytes_accessed=4 * depth * width, transcendentals=0
        ),
        name="base",
    )(*x_parts, gate_matrix, up_matrix, *heads)


def finish_kernel(step, gate_ref, up_ref, pick_ref, order_ref, *refs):
    rows_refs, (out_ref, held, sems) = refs[:-3], refs[-3:]
    writes = []
    for n in range(gate_ref.shape[1] // step):
        at = slice(n * step, (n + 1) * step)
        stacked = jnp.concatenate([ref[:, at] for ref in rows_refs], axis=0)
        gate = gate_ref[:, at] + jnp.dot(pick_ref[...], stacked, preferred_element_type=F32)
        hidden = (gate / (1.0 + jnp.exp(-gate)) * up_ref[:, at]).astype(BF16)
        held[:, at] = jnp.dot(order_ref[...], hidden, preferred_element_type=F32).astype(BF16)
        writes.append(pltpu.make_async_copy(held.at[:, at], out_ref.at[:, at], sems.at[n]))
        writes[-1].start()
    for copy in writes:
        copy.wait()


def finish(gate, up, pick, order, rows_by_plane):
    total, width = gate.shape
    n = 2 if width % (2 * LANES) == 0 else 1
    return pl.pallas_call(
        functools.partial(finish_kernel, width // n),
        out_shape=pltpu.HBM((total, width), BF16),
        in_specs=[VMEM] * (4 + len(rows_by_plane)),
        out_specs=HBM,
        scratch_shapes=[pltpu.VMEM((total, width), BF16), pltpu.SemaphoreType.DMA((n,))],
        compiler_params=pltpu.CompilerParams(vmem_limit_bytes=8 * 1024 * 1024),
        cost_estimate=pl.CostEstimate(flops=0, bytes_accessed=4 * total * width * 4, transcendentals=total * width),
        name="finish",
    )(gate, up, pick, order, *rows_by_plane)


def plane_shards(
    tokens,
    token_adapter_index,
    adapter_slot_index,
    gate_matrix,
    up_matrix,
    adapter_down_factor,
    adapter_up_factor,
):
    count = lax.axis_size("dp")
    me, y = lax.axis_index("dp"), lax.axis_index("groups")
    z = me // 4
    up_factor, gate_matrix, up_matrix = (
        pltpu.with_memory_space_constraint(v, pltpu.HBM) for v in (adapter_up_factor[0], gate_matrix, up_matrix)
    )
    own_rows, depth = tokens.shape
    total = own_rows * count
    width = gate_matrix.shape[1]
    rank = adapter_up_factor.shape[1]

    def swap(value, k):
        return lax.ppermute(value, "dp", [(d, d ^ k) for d in range(count)])

    def other(value):
        return lax.ppermute(value, "groups", [(0, 1), (1, 0)])

    ids = jnp.broadcast_to(token_adapter_index.astype(BF16), (own_rows, LANES))
    packed = jnp.concatenate([tokens, ids], axis=1)
    packed, cross, both = lax.optimization_barrier((packed, *cut_cross(up_factor, width)))
    cross, both = swap(cross, 2), swap(both, 3)
    second, third = swap(packed, 8), swap(packed, 12)
    pair = jnp.concatenate([packed, swap(packed, 2)], axis=0)
    remote = jnp.concatenate([second, third], axis=0)
    own_chip, own_plane, core_chip, core_plane = repack(up_factor, width)
    core_chip, core_plane = swap(core_chip, 1), swap(core_plane, 1)
    gate_head = fetch(own_plane, gate_matrix)
    pair, remote, down, core_chip, core_plane, gate_head = lax.optimization_barrier(
        (pair, remote, adapter_down_factor[0], core_chip, core_plane, gate_head)
    )
    close = jnp.concatenate([pair, swap(pair, 4)], axis=0)
    remote = jnp.concatenate([remote, swap(remote, 2)], axis=0)
    up_head = fetch(pair, up_matrix)
    cross, both, up_head = lax.optimization_barrier((cross, both, up_head))
    crossed = jnp.concatenate([cross, both], axis=0)
    heads = (gate_head, up_head)
    close, remote, heads = lax.optimization_barrier((close, remote, heads))
    x_parts = (close, remote, swap(close, 1), swap(remote, 1))
    distances = [0, 2, 4, 6, 8, 12, 10, 14]
    distances = distances + [k + 1 for k in distances]

    cross_parts = (crossed, other(crossed))
    half = rank // 2

    distance = jnp.array([k for k in distances for _ in range(own_rows)], jnp.int32)
    table = jnp.pad(adapter_slot_index, (0, LANES - count))[None, :]
    low, meta, first, order, rounds = low_rows(x_parts, down.T, table, distance)
    planes, ranks = meta[0], meta[1]

    chip_plan = tuple(((0, i, 0, rank), (1, i, 0, rank)) for i in range(2 * len(ROWS)))
    plane_plan = tuple(
        ((0, i, 0, rank), (1, i, 0, rank)) + tuple((n, i, at, half) for at in (0, half) for n in (2, 3))
        for i in range(len(FACTORS))
    )

    def chip_rows(e):
        return delta_rows(e, (own_chip, core_chip), chip_plan, width)

    def plane_rows(e):
        return delta_rows(e, (own_plane, core_plane, *cross_parts), plane_plan, width)

    def arrived(chip, plane):
        here, first, here_cross, first_cross = chip
        second, third = plane
        return [here, swap(first, 4), swap(second, 8), swap(third, 12), swap(here_cross, 2), swap(first_cross, 6)]

    cross_low, both_low = swap(low, 2), swap(low, 3)
    chip = jnp.concatenate([low, swap(low, 1)], axis=1)
    by_chip = chip_rows(chip[: ROOMS[0]])
    by_chip, cross_low, both_low = lax.optimization_barrier((by_chip, cross_low, both_low))
    plane = jnp.concatenate([chip, cross_low, both_low], axis=1)
    by_plane = plane_rows(plane[: ROOMS[0]])
    by_plane, x_parts = lax.optimization_barrier((by_plane, x_parts))
    rows = arrived(by_chip, by_plane)
    gate, up = base(x_parts, gate_matrix, up_matrix, heads)

    def picked(start, room):
        at = jnp.where((ranks >= start) & (ranks < start + room), planes * room + ranks - start, -1)
        pick = (at[:, None] == jnp.arange(PLANES * room, dtype=jnp.int32)[None, :]).astype(BF16)
        return jnp.concatenate([pick, pick[:, : len(ROWS) * room]], axis=1)

    def short():
        return finish(gate, up, first, order, rows)

    def more(room):
        at = slice(ROOMS[0], ROOMS[0] + room)
        rest = arrived(chip_rows(chip[at]), plane_rows(plane[at]))
        pick = jnp.concatenate([first, picked(ROOMS[0], room)], axis=1)
        return finish(gate, up, pick, order, rows + rest)

    return lax.switch(rounds[0], (short, lambda: more(ROOMS[1]), lambda: more(ROOMS[1] + ROOMS[2])))


def solution(mesh):
    in_specs = (
        P(("groups", "dp"), None),
        P(("groups", "dp"), None),
        P(),
        P(None, "dp"),
        P(None, "dp"),
        P("dp", None, None),
        P("dp", None, None),
    )
    out_specs = P("groups", "dp")
    shards = plane_shards if mesh.shape["dp"] == 16 and mesh.shape["groups"] == 2 else general_shards
    return jax.shard_map(shards, mesh=mesh, in_specs=in_specs, out_specs=out_specs, check_vma=False)
```

```python
import functools

import jax
import jax.numpy as jnp
from jax import lax
from jax.experimental import pallas as pl
from jax.experimental.pallas import tpu as pltpu
from jax.sharding import PartitionSpec as P

CAP = 32
LANES = 128
PLANES = 4
F32 = jnp.float32
BF16 = jnp.bfloat16


def general_shards(
    tokens,
    token_adapter_index,
    adapter_slot_index,
    gate_matrix,
    up_matrix,
    adapter_down_factor,
    adapter_up_factor,
):
    count = lax.axis_size("dp")
    myself = lax.axis_index("dp")
    all_rows, all_ids = (
        lax.all_gather(tokens, "dp", axis=0, tiled=True),
        lax.all_gather(token_adapter_index, "dp", axis=0, tiled=True),
    )
    total = all_rows.shape[0]
    places = jnp.arange(count, dtype=jnp.int32)
    match = all_ids[:, 0][:, None] == places[None, :]
    slots = jnp.sum(jnp.where(match, adapter_slot_index[None, :], 0), 1)
    slot_match = slots[:, None] == places[None, :]
    onehot = slot_match.astype(jnp.int32)
    ranks = jnp.sum(jnp.cumsum(onehot, 0) * onehot, 1) - 1
    capacity = CAP
    columns = jnp.arange(capacity, dtype=jnp.int32)
    mine = (slots == myself)[:, None] & (ranks[:, None] == columns[None, :])
    row_list = jnp.sum(jnp.where(mine, jnp.arange(total, dtype=jnp.int32)[:, None], 0), 0)
    selected_slot = jnp.take(all_rows, row_list, axis=0)
    reduced_rows = jnp.dot(
        selected_slot, adapter_down_factor[0], preferred_element_type=F32
    ).astype(BF16)
    slot_pieces = lax.all_to_all(adapter_up_factor, "dp", split_axis=2, concat_axis=0, tiled=True)
    all_low = lax.all_gather(reduced_rows, "dp", axis=0, tiled=True)
    rank_width = all_low.shape[1]
    token_low = jnp.take(all_low, slots * capacity + ranks, axis=0)
    expanded = (token_low[:, None, :] * slot_match.astype(BF16)[:, :, None]).reshape(
        total, count * rank_width
    )
    stacked = slot_pieces.reshape(count * rank_width, slot_pieces.shape[2])
    delta = jnp.dot(expanded, stacked, preferred_element_type=F32).astype(BF16)
    gate_base = jnp.dot(all_rows, gate_matrix, preferred_element_type=F32)
    up = jnp.dot(all_rows, up_matrix, preferred_element_type=F32)
    gate = gate_base + delta.astype(F32)
    return (jax.nn.silu(gate) * up).astype(BF16)


ANY = pl.BlockSpec(memory_space=pl.ANY)
HBM = pl.BlockSpec(memory_space=pltpu.HBM)
VMEM = pl.BlockSpec(memory_space=pltpu.VMEM)
ROOMS = (64, 16, 48)
FACTORS = (2, 3)
ROWS = (0, 1)


def cut(u_ref, sems, width, wanted):
    rank = u_ref.shape[0]
    half = rank // 2
    z = lax.axis_index("dp") // 4
    copies = []
    for n, (j, x, c, part, target) in enumerate(wanted):
        at = pl.multiple_of(((lax.bitwise_xor(z, j) * 2 + x) * 2 + c) * width, LANES)
        rows = pl.ds(0, rank) if part is None else pl.ds(pl.multiple_of(part * half, half), half)
        copies.append(pltpu.make_async_copy(u_ref.at[rows, pl.ds(at, width)], target, sems.at[n]))
    for copy in copies:
        copy.start()
    for copy in copies:
        copy.wait()


def position():
    me = lax.axis_index("dp")
    return (me // 2) % 2, me % 2


def cross_kernel(width, u_ref, cross_ref, both_ref, sems):
    (x, c), y = position(), lax.axis_index("groups")
    wanted = []
    for i, j in enumerate(FACTORS):
        place = pl.ds(i * width, width)
        wanted += [(j, 1 - x, c, y, cross_ref.at[:, place]), (j, 1 - x, 1 - c, y, both_ref.at[:, place])]
    cut(u_ref, sems, width, wanted)


def cut_cross(u, width):
    rank = u.shape[0]
    n = 2 * len(FACTORS)
    split = pltpu.VMEM((rank // 2, len(FACTORS) * width), BF16)
    return pl.pallas_call(
        functools.partial(cross_kernel, width),
        out_shape=[split, split],
        in_specs=[HBM],
        out_specs=[VMEM, VMEM],
        scratch_shapes=[pltpu.SemaphoreType.DMA((n,))],
        compiler_params=pltpu.CompilerParams(vmem_limit_bytes=4 * 1024 * 1024),
        cost_estimate=pl.CostEstimate(flops=0, bytes_accessed=2 * rank * n * width, transcendentals=0),
        name="cut_cross",
    )(u)


def repack_kernel(width, u_ref, own_rows_ref, own_ref, core_rows_ref, core_ref, sems):
    x, c = position()
    wanted = []
    for cc, rows_ref, ref in ((1 - c, core_rows_ref, core_ref), (c, own_rows_ref, own_ref)):
        for target, blocks in (
            (ref, [(j, x) for j in FACTORS]),
            (rows_ref, [(j, xx) for xx in (x, 1 - x) for j in ROWS]),
        ):
            for i, (j, xx) in enumerate(blocks):
                wanted.append((j, xx, cc, None, target.at[:, pl.ds(i * width, width)]))
    cut(u_ref, sems, width, wanted)


def repack(u, width):
    rank = u.shape[0]
    n = 2 * (len(FACTORS) + 2 * len(ROWS))
    for_rows = pltpu.VMEM((rank, 2 * len(ROWS) * width), BF16)
    for_factors = pltpu.VMEM((rank, len(FACTORS) * width), BF16)
    return pl.pallas_call(
        functools.partial(repack_kernel, width),
        out_shape=[for_rows, for_factors] * 2,
        in_specs=[HBM],
        out_specs=[VMEM] * 4,
        scratch_shapes=[pltpu.SemaphoreType.DMA((n,))],
        compiler_params=pltpu.CompilerParams(vmem_limit_bytes=4 * 1024 * 1024),
        cost_estimate=pl.CostEstimate(flops=0, bytes_accessed=3 * u.size, transcendentals=0),
        name="repack",
    )(u)


def low_kernel(*refs):
    x_refs, (down_ref, table_ref, distance_ref, distance_column_ref), outs = refs[:4], refs[4:8], refs[8:]
    low_ref, meta_ref, pick_ref, order_ref, rounds_ref = outs
    depth = down_ref.shape[1]
    x = jnp.concatenate([ref[:, :depth] for ref in x_refs], axis=0)
    low = lax.dot_general(x, down_ref[...], (((1,), (1,)), ((), ())), preferred_element_type=F32).astype(BF16)
    ids = jnp.concatenate([ref[:, depth:] for ref in x_refs], axis=0).astype(F32)
    total = ids.shape[0]
    lane = lax.broadcasted_iota(jnp.int32, ids.shape, 1).astype(F32)
    place = lax.broadcasted_iota(jnp.int32, ids.shape, 0).astype(F32)
    table = jnp.broadcast_to(table_ref[...], ids.shape).astype(F32)
    slots = jnp.broadcast_to(jnp.sum(jnp.where(ids == lane, table, 0.0), axis=1, keepdims=True), (total, total))
    slots_row = slots.T
    planes, planes_row = jnp.floor(slots * 0.25), jnp.floor(slots_row * 0.25)
    me = lax.axis_index("dp")
    own_rows = total // lax.axis_size("dp")

    def rows_at(distance, along):
        inner = lax.broadcasted_iota(jnp.int32, ids.shape, along) % own_rows
        owner = lax.bitwise_xor(jnp.broadcast_to(distance, ids.shape), jnp.broadcast_to(me, ids.shape))
        return (owner * own_rows + inner).astype(F32)

    at, at_column = rows_at(distance_ref[...], 1), rows_at(distance_column_ref[...], 0)
    same = planes == planes_row
    ranks_row = jnp.sum(jnp.where(same & (at_column < at), 1.0, 0.0), axis=0, keepdims=True)
    ranks = jnp.sum(jnp.where(same & (at < at_column), 1.0, 0.0), axis=1, keepdims=True)
    mine = jnp.where((slots_row == me.astype(F32)) & (ranks_row == place), 1.0, 0.0).astype(BF16)
    low_ref[...] = jnp.dot(mine, low, preferred_element_type=F32).astype(BF16)
    z = jnp.broadcast_to(me // 4, (1, total))
    meta_ref[0:1, :] = lax.bitwise_xor(planes_row[0:1, :].astype(jnp.int32), z)
    meta_ref[1:2, :] = ranks_row.astype(jnp.int32)
    order_ref[...] = jnp.where(at == place, 1.0, 0.0).astype(BF16)
    room = ROOMS[0]
    wide = lax.broadcasted_iota(jnp.int32, pick_ref.shape, 1)
    block = wide // room
    distance = jnp.where(block < PLANES, block, block - PLANES)
    wanted = lax.bitwise_xor(distance, jnp.broadcast_to(me // 4, distance.shape)).astype(F32)
    found = (planes[:, :1] == wanted) & (ranks == (wide % room).astype(F32))
    pick_ref[...] = jnp.where(found, 1.0, 0.0).astype(BF16)
    most = jnp.max(ranks_row)
    rounds_ref[0] = (most >= room).astype(jnp.int32) + (most >= room + ROOMS[1]).astype(jnp.int32)


def low_rows(x_parts, down, table, distance):
    total = distance.shape[0]
    rank = down.shape[0]
    return pl.pallas_call(
        low_kernel,
        out_shape=[
            jax.ShapeDtypeStruct((total, rank), BF16),
            jax.ShapeDtypeStruct((2, total), jnp.int32),
            jax.ShapeDtypeStruct((total, (PLANES + len(ROWS)) * ROOMS[0]), BF16),
            jax.ShapeDtypeStruct((total, total), BF16),
            jax.ShapeDtypeStruct((1,), jnp.int32),
        ],
        in_specs=[VMEM] * 8,
        out_specs=[VMEM] * 4 + [pl.BlockSpec(memory_space=pltpu.SMEM)],
        compiler_params=pltpu.CompilerParams(vmem_limit_bytes=8 * 1024 * 1024),
        cost_estimate=pl.CostEstimate(flops=0, bytes_accessed=4096, transcendentals=0),
        name="low_rows",
    )(*x_parts, down, table, distance[None, :], distance[:, None])


def delta_kernel(plan, width, e_ref, *refs):
    parts, outs = refs[: len(refs) - len(plan)], refs[len(refs) - len(plan) :]
    e = e_ref[...]
    chip = 2 * parts[0].shape[0]
    if e.shape[1] > chip:
        parts = (*parts[:-2], jnp.concatenate([parts[-2][...], parts[-1][...]], axis=1))
        shape = (e.shape[1] - chip,) * 2
        half = jnp.broadcast_to(lax.axis_index("groups") * (chip // 4), shape)
        here, there = lax.broadcasted_iota(jnp.int32, shape, 0), lax.broadcasted_iota(jnp.int32, shape, 1)
        turn = jnp.where(lax.bitwise_xor(here, half) == there, 1.0, 0.0).astype(BF16)
        beyond = jnp.dot(e[:, chip:], turn, preferred_element_type=F32).astype(BF16)
        e = jnp.concatenate([e[:, :chip], beyond], axis=1)
    for pieces, out in zip(plan, outs):
        stacked = jnp.concatenate(
            [parts[n][at : at + rows, i * width : (i + 1) * width] for n, i, at, rows in pieces], axis=0
        )
        out[...] = jnp.dot(e[:, : stacked.shape[0]], stacked, preferred_element_type=F32).astype(BF16)


def delta_rows(e, parts, plan, width):
    rows = e.shape[0]
    n = len(plan)
    return pl.pallas_call(
        functools.partial(delta_kernel, plan, width),
        out_shape=[jax.ShapeDtypeStruct((rows, width), BF16)] * n,
        in_specs=[VMEM] * (1 + len(parts)),
        out_specs=[VMEM] * n,
        compiler_params=pltpu.CompilerParams(vmem_limit_bytes=8 * 1024 * 1024),
        cost_estimate=pl.CostEstimate(flops=0, bytes_accessed=4096, transcendentals=0),
        name="delta_rows",
    )(e, *parts)


BLOCK = 512
SLOTS = 3
AHEAD = 4


def fetch_kernel(first, after_ref, ref, head_ref, sem):
    copy = pltpu.make_async_copy(ref.at[pl.ds(first, head_ref.shape[0])], head_ref, sem)
    copy.start()
    copy.wait()


def fetch(after, matrix):
    shape = jax.ShapeDtypeStruct((AHEAD * BLOCK, matrix.shape[1]), BF16)
    return pl.pallas_call(
        functools.partial(fetch_kernel, 0),
        out_shape=shape,
        in_specs=[ANY, HBM],
        out_specs=VMEM,
        scratch_shapes=[pltpu.SemaphoreType.DMA],
        compiler_params=pltpu.CompilerParams(vmem_limit_bytes=4 * 1024 * 1024),
        cost_estimate=pl.CostEstimate(flops=0, bytes_accessed=8 * shape.size, transcendentals=0),
        name="fetch",
    )(after, matrix)


def base_kernel(steps, rows, *refs):
    x_refs, (g_ref, u_ref, g_head, u_head), refs = refs[:4], refs[4:8], refs[8:]
    gate_ref, up_ref, x_held, g_held, u_held, x_sems, g_sems, u_sems = refs

    def weights(k, slot):
        at = pl.ds(pl.multiple_of(k * BLOCK, BLOCK), BLOCK)
        return (
            pltpu.make_async_copy(g_ref.at[at], g_held.at[slot], g_sems.at[slot]),
            pltpu.make_async_copy(u_ref.at[at], u_held.at[slot], u_sems.at[slot]),
        )

    columns = pl.ds(0, steps * BLOCK)
    loads = [
        pltpu.make_async_copy(ref.at[:, columns], x_held.at[pl.ds(i * rows, rows)], x_sems.at[i])
        for i, ref in enumerate(x_refs)
    ]
    for copy in loads:
        copy.start()
    for k in range(SLOTS):
        for copy in weights(AHEAD + k, k):
            copy.start()
    for copy in loads:
        copy.wait()
    x = x_held[:, : AHEAD * BLOCK]
    gate_ref[...] = jnp.dot(x, g_head[...], preferred_element_type=F32)
    up_ref[...] = jnp.dot(x, u_head[...], preferred_element_type=F32)

    def step(n, carry):
        slot = lax.rem(n, SLOTS)
        k = n + AHEAD
        gate_copy, up_copy = weights(k, slot)
        x = x_held[:, pl.ds(pl.multiple_of(k * BLOCK, BLOCK), BLOCK)]
        gate_copy.wait()
        gate_ref[...] += jnp.dot(x, g_held[slot], preferred_element_type=F32)
        up_copy.wait()
        up_ref[...] += jnp.dot(x, u_held[slot], preferred_element_type=F32)

        @pl.when(k + SLOTS < steps)
        def _():
            for copy in weights(k + SLOTS, slot):
                copy.start()

        return carry

    lax.fori_loop(0, steps - AHEAD, step, 0)


def base(x_parts, gate_matrix, up_matrix, heads):
    depth, width = gate_matrix.shape
    steps = depth // BLOCK
    rows = x_parts[0].shape[0]
    total = rows * len(x_parts)
    shape = jax.ShapeDtypeStruct((total, width), F32)
    return pl.pallas_call(
        functools.partial(base_kernel, steps, rows),
        out_shape=[shape, shape],
        in_specs=[ANY] * len(x_parts) + [HBM] * 2 + [VMEM] * 2,
        out_specs=[VMEM, VMEM],
        scratch_shapes=[
            pltpu.VMEM((total, depth), BF16),
            pltpu.VMEM((SLOTS, BLOCK, width), BF16),
            pltpu.VMEM((SLOTS, BLOCK, width), BF16),
            pltpu.SemaphoreType.DMA((len(x_parts),)),
            pltpu.SemaphoreType.DMA((SLOTS,)),
            pltpu.SemaphoreType.DMA((SLOTS,)),
        ],
        compiler_params=pltpu.CompilerParams(vmem_limit_bytes=18 * 1024 * 1024),
        cost_estimate=pl.CostEstimate(
            flops=4 * total * depth * width, bytes_accessed=4 * depth * width, transcendentals=0
        ),
        name="base",
    )(*x_parts, gate_matrix, up_matrix, *heads)


def finish_kernel(step, gate_ref, up_ref, pick_ref, order_ref, *refs):
    rows_refs, (out_ref, held, sems) = refs[:-3], refs[-3:]
    writes = []
    for n in range(gate_ref.shape[1] // step):
        at = slice(n * step, (n + 1) * step)
        stacked = jnp.concatenate([ref[:, at] for ref in rows_refs], axis=0)
        gate = gate_ref[:, at] + jnp.dot(pick_ref[...], stacked, preferred_element_type=F32)
        hidden = (gate / (1.0 + jnp.exp(-gate)) * up_ref[:, at]).astype(BF16)
        held[:, at] = jnp.dot(order_ref[...], hidden, preferred_element_type=F32).astype(BF16)
        writes.append(pltpu.make_async_copy(held.at[:, at], out_ref.at[:, at], sems.at[n]))
        writes[-1].start()
    for copy in writes:
        copy.wait()


def finish(gate, up, pick, order, rows_by_plane):
    total, width = gate.shape
    n = 2 if width % (2 * LANES) == 0 else 1
    return pl.pallas_call(
        functools.partial(finish_kernel, width // n),
        out_shape=pltpu.HBM((total, width), BF16),
        in_specs=[VMEM] * (4 + len(rows_by_plane)),
        out_specs=HBM,
        scratch_shapes=[pltpu.VMEM((total, width), BF16), pltpu.SemaphoreType.DMA((n,))],
        compiler_params=pltpu.CompilerParams(vmem_limit_bytes=8 * 1024 * 1024),
        cost_estimate=pl.CostEstimate(flops=0, bytes_accessed=4 * total * width * 4, transcendentals=total * width),
        name="finish",
    )(gate, up, pick, order, *rows_by_plane)


def plane_shards(
    tokens,
    token_adapter_index,
    adapter_slot_index,
    gate_matrix,
    up_matrix,
    adapter_down_factor,
    adapter_up_factor,
):
    count = lax.axis_size("dp")
    me, y = lax.axis_index("dp"), lax.axis_index("groups")
    z = me // 4
    up_factor, gate_matrix, up_matrix = (
        pltpu.with_memory_space_constraint(v, pltpu.HBM) for v in (adapter_up_factor[0], gate_matrix, up_matrix)
    )
    own_rows, depth = tokens.shape
    total = own_rows * count
    width = gate_matrix.shape[1]
    rank = adapter_up_factor.shape[1]

    def swap(value, k):
        return lax.ppermute(value, "dp", [(d, d ^ k) for d in range(count)])

    def other(value):
        return lax.ppermute(value, "groups", [(0, 1), (1, 0)])

    index, cross, both = lax.optimization_barrier((token_adapter_index, *cut_cross(up_factor, width)))
    ids = jnp.broadcast_to(index.astype(BF16), (own_rows, LANES))
    packed = jnp.concatenate([tokens, ids], axis=1)
    cross, both = swap(cross, 2), swap(both, 3)
    second, third = swap(packed, 8), swap(packed, 12)
    pair = jnp.concatenate([packed, swap(packed, 2)], axis=0)
    remote = jnp.concatenate([second, third], axis=0)
    own_chip, own_plane, core_chip, core_plane = repack(up_factor, width)
    gate_head = fetch(own_plane, gate_matrix)
    close = jnp.concatenate([pair, swap(pair, 4)], axis=0)
    remote, down, core_chip, core_plane, gate_head, cross, both = lax.optimization_barrier(
        (remote, adapter_down_factor[0], core_chip, core_plane, gate_head, cross, both)
    )
    crossed = jnp.concatenate([cross, both], axis=0)
    part = width * 3 // 7 // LANES * LANES
    from_group = other(crossed[:, :part])
    remote = jnp.concatenate([remote, swap(remote, 2)], axis=0)
    core_chip, core_plane = swap(core_chip, 1), swap(core_plane, 1)
    heads = (gate_head, fetch(crossed, up_matrix))
    close, remote, heads, from_group = lax.optimization_barrier((close, remote, heads, from_group))
    x_parts = (close, remote, swap(close, 1), swap(remote, 1))
    distances = [0, 2, 4, 6, 8, 12, 10, 14]
    distances = distances + [k + 1 for k in distances]

    cross_parts = (crossed, from_group, other(crossed[:, part:]))
    half = rank // 2

    distance = jnp.array([k for k in distances for _ in range(own_rows)], jnp.int32)
    table = jnp.pad(adapter_slot_index, (0, LANES - count))[None, :]
    low, meta, first, order, rounds = low_rows(x_parts, down.T, table, distance)
    planes, ranks = meta[0], meta[1]

    chip_plan = tuple(((0, i, 0, rank), (1, i, 0, rank)) for i in range(2 * len(ROWS)))
    plane_plan = tuple(
        ((0, i, 0, rank), (1, i, 0, rank)) + tuple((n, i, at, half) for at in (0, half) for n in (2, 3))
        for i in range(len(FACTORS))
    )

    def chip_rows(e):
        return delta_rows(e, (own_chip, core_chip), chip_plan, width)

    def plane_rows(e):
        return delta_rows(e, (own_plane, core_plane, *cross_parts), plane_plan, width)

    def arrived(chip, plane):
        here, first, here_cross, first_cross = chip
        second, third = plane
        return [here, swap(first, 4), swap(second, 8), swap(third, 12), swap(here_cross, 2), swap(first_cross, 6)]

    cross_low, both_low = swap(low, 2), swap(low, 3)
    chip = jnp.concatenate([low, swap(low, 1)], axis=1)
    by_chip = chip_rows(chip[: ROOMS[0]])
    by_chip, cross_low, both_low = lax.optimization_barrier((by_chip, cross_low, both_low))
    plane = jnp.concatenate([chip, cross_low, both_low], axis=1)
    by_plane = plane_rows(plane[: ROOMS[0]])
    by_plane, by_chip, x_parts = lax.optimization_barrier((by_plane, by_chip, x_parts))
    rows = arrived(by_chip, by_plane)
    gate, up = base(x_parts, gate_matrix, up_matrix, heads)

    def picked(start, room):
        at = jnp.where((ranks >= start) & (ranks < start + room), planes * room + ranks - start, -1)
        pick = (at[:, None] == jnp.arange(PLANES * room, dtype=jnp.int32)[None, :]).astype(BF16)
        return jnp.concatenate([pick, pick[:, : len(ROWS) * room]], axis=1)

    def short():
        return finish(gate, up, first, order, rows)

    def more(room):
        at = slice(ROOMS[0], ROOMS[0] + room)
        rest = arrived(chip_rows(chip[at]), plane_rows(plane[at]))
        pick = jnp.concatenate([first, picked(ROOMS[0], room)], axis=1)
        return finish(gate, up, pick, order, rows + rest)

    return lax.switch(rounds[0], (short, lambda: more(ROOMS[1]), lambda: more(ROOMS[1] + ROOMS[2])))


def solution(mesh):
    in_specs = (
        P(("groups", "dp"), None),
        P(("groups", "dp"), None),
        P(),
        P(None, "dp"),
        P(None, "dp"),
        P("dp", None, None),
        P("dp", None, None),
    )
    out_specs = P("groups", "dp")
    shards = plane_shards if mesh.shape["dp"] == 16 and mesh.shape["groups"] == 2 else general_shards
    return jax.shard_map(shards, mesh=mesh, in_specs=in_specs, out_specs=out_specs, check_vma=False)
```

```python
import functools

import jax
import jax.numpy as jnp
from jax import lax
from jax.experimental import pallas as pl
from jax.experimental.pallas import tpu as pltpu
from jax.sharding import PartitionSpec as P

CAP = 32
LANES = 128
PLANES = 4
F32 = jnp.float32
BF16 = jnp.bfloat16


def general_shards(
    tokens,
    token_adapter_index,
    adapter_slot_index,
    gate_matrix,
    up_matrix,
    adapter_down_factor,
    adapter_up_factor,
):
    count = lax.axis_size("dp")
    myself = lax.axis_index("dp")
    all_rows, all_ids = (
        lax.all_gather(tokens, "dp", axis=0, tiled=True),
        lax.all_gather(token_adapter_index, "dp", axis=0, tiled=True),
    )
    total = all_rows.shape[0]
    places = jnp.arange(count, dtype=jnp.int32)
    match = all_ids[:, 0][:, None] == places[None, :]
    slots = jnp.sum(jnp.where(match, adapter_slot_index[None, :], 0), 1)
    slot_match = slots[:, None] == places[None, :]
    onehot = slot_match.astype(jnp.int32)
    ranks = jnp.sum(jnp.cumsum(onehot, 0) * onehot, 1) - 1
    capacity = CAP
    columns = jnp.arange(capacity, dtype=jnp.int32)
    mine = (slots == myself)[:, None] & (ranks[:, None] == columns[None, :])
    row_list = jnp.sum(jnp.where(mine, jnp.arange(total, dtype=jnp.int32)[:, None], 0), 0)
    selected_slot = jnp.take(all_rows, row_list, axis=0)
    reduced_rows = jnp.dot(
        selected_slot, adapter_down_factor[0], preferred_element_type=F32
    ).astype(BF16)
    slot_pieces = lax.all_to_all(adapter_up_factor, "dp", split_axis=2, concat_axis=0, tiled=True)
    all_low = lax.all_gather(reduced_rows, "dp", axis=0, tiled=True)
    rank_width = all_low.shape[1]
    token_low = jnp.take(all_low, slots * capacity + ranks, axis=0)
    expanded = (token_low[:, None, :] * slot_match.astype(BF16)[:, :, None]).reshape(
        total, count * rank_width
    )
    stacked = slot_pieces.reshape(count * rank_width, slot_pieces.shape[2])
    delta = jnp.dot(expanded, stacked, preferred_element_type=F32).astype(BF16)
    gate_base = jnp.dot(all_rows, gate_matrix, preferred_element_type=F32)
    up = jnp.dot(all_rows, up_matrix, preferred_element_type=F32)
    gate = gate_base + delta.astype(F32)
    return (jax.nn.silu(gate) * up).astype(BF16)


ANY = pl.BlockSpec(memory_space=pl.ANY)
HBM = pl.BlockSpec(memory_space=pltpu.HBM)
VMEM = pl.BlockSpec(memory_space=pltpu.VMEM)
ROOMS = (64, 16, 48)
FACTORS = (2, 3)
ROWS = (0, 1)


def cut(u_ref, sems, width, wanted):
    rank = u_ref.shape[0]
    half = rank // 2
    z = lax.axis_index("dp") // 4
    copies = []
    for n, (j, x, c, part, target) in enumerate(wanted):
        at = pl.multiple_of(((lax.bitwise_xor(z, j) * 2 + x) * 2 + c) * width, LANES)
        rows = pl.ds(0, rank) if part is None else pl.ds(pl.multiple_of(part * half, half), half)
        copies.append(pltpu.make_async_copy(u_ref.at[rows, pl.ds(at, width)], target, sems.at[n]))
    for copy in copies:
        copy.start()
    for copy in copies:
        copy.wait()


def position():
    me = lax.axis_index("dp")
    return (me // 2) % 2, me % 2


def cross_kernel(width, u_ref, cross_ref, both_ref, sems):
    (x, c), y = position(), lax.axis_index("groups")
    wanted = []
    for i, j in enumerate(FACTORS):
        place = pl.ds(i * width, width)
        wanted += [(j, 1 - x, c, y, cross_ref.at[:, place]), (j, 1 - x, 1 - c, y, both_ref.at[:, place])]
    cut(u_ref, sems, width, wanted)


def cut_cross(u, width):
    rank = u.shape[0]
    n = 2 * len(FACTORS)
    split = pltpu.VMEM((rank // 2, len(FACTORS) * width), BF16)
    return pl.pallas_call(
        functools.partial(cross_kernel, width),
        out_shape=[split, split],
        in_specs=[HBM],
        out_specs=[VMEM, VMEM],
        scratch_shapes=[pltpu.SemaphoreType.DMA((n,))],
        compiler_params=pltpu.CompilerParams(vmem_limit_bytes=4 * 1024 * 1024),
        cost_estimate=pl.CostEstimate(flops=0, bytes_accessed=2 * rank * n * width, transcendentals=0),
        name="cut_cross",
    )(u)


def repack_kernel(width, u_ref, own_rows_ref, own_ref, core_rows_ref, core_ref, sems):
    x, c = position()
    wanted = []
    for cc, rows_ref, ref in ((1 - c, core_rows_ref, core_ref), (c, own_rows_ref, own_ref)):
        for target, blocks in (
            (ref, [(j, x) for j in FACTORS]),
            (rows_ref, [(j, xx) for xx in (x, 1 - x) for j in ROWS]),
        ):
            for i, (j, xx) in enumerate(blocks):
                wanted.append((j, xx, cc, None, target.at[:, pl.ds(i * width, width)]))
    cut(u_ref, sems, width, wanted)


def repack(u, width):
    rank = u.shape[0]
    n = 2 * (len(FACTORS) + 2 * len(ROWS))
    for_rows = pltpu.VMEM((rank, 2 * len(ROWS) * width), BF16)
    for_factors = pltpu.VMEM((rank, len(FACTORS) * width), BF16)
    return pl.pallas_call(
        functools.partial(repack_kernel, width),
        out_shape=[for_rows, for_factors] * 2,
        in_specs=[HBM],
        out_specs=[VMEM] * 4,
        scratch_shapes=[pltpu.SemaphoreType.DMA((n,))],
        compiler_params=pltpu.CompilerParams(vmem_limit_bytes=4 * 1024 * 1024),
        cost_estimate=pl.CostEstimate(flops=0, bytes_accessed=3 * u.size, transcendentals=0),
        name="repack",
    )(u)


def low_kernel(*refs):
    x_refs, (down_ref, table_ref, distance_ref, distance_column_ref), outs = refs[:4], refs[4:8], refs[8:]
    low_ref, meta_ref, pick_ref, order_ref, rounds_ref = outs
    depth = down_ref.shape[1]
    x = jnp.concatenate([ref[:, :depth] for ref in x_refs], axis=0)
    low = lax.dot_general(x, down_ref[...], (((1,), (1,)), ((), ())), preferred_element_type=F32).astype(BF16)
    ids = jnp.concatenate([ref[:, depth:] for ref in x_refs], axis=0).astype(F32)
    total = ids.shape[0]
    lane = lax.broadcasted_iota(jnp.int32, ids.shape, 1).astype(F32)
    place = lax.broadcasted_iota(jnp.int32, ids.shape, 0).astype(F32)
    table = jnp.broadcast_to(table_ref[...], ids.shape).astype(F32)
    slots = jnp.broadcast_to(jnp.sum(jnp.where(ids == lane, table, 0.0), axis=1, keepdims=True), (total, total))
    slots_row = slots.T
    planes, planes_row = jnp.floor(slots * 0.25), jnp.floor(slots_row * 0.25)
    me = lax.axis_index("dp")
    own_rows = total // lax.axis_size("dp")

    def rows_at(distance, along):
        inner = lax.broadcasted_iota(jnp.int32, ids.shape, along) % own_rows
        owner = lax.bitwise_xor(jnp.broadcast_to(distance, ids.shape), jnp.broadcast_to(me, ids.shape))
        return (owner * own_rows + inner).astype(F32)

    at, at_column = rows_at(distance_ref[...], 1), rows_at(distance_column_ref[...], 0)
    same = planes == planes_row
    ranks_row = jnp.sum(jnp.where(same & (at_column < at), 1.0, 0.0), axis=0, keepdims=True)
    ranks = jnp.sum(jnp.where(same & (at < at_column), 1.0, 0.0), axis=1, keepdims=True)
    mine = jnp.where((slots_row == me.astype(F32)) & (ranks_row == place), 1.0, 0.0).astype(BF16)
    low_ref[...] = jnp.dot(mine, low, preferred_element_type=F32).astype(BF16)
    z = jnp.broadcast_to(me // 4, (1, total))
    meta_ref[0:1, :] = lax.bitwise_xor(planes_row[0:1, :].astype(jnp.int32), z)
    meta_ref[1:2, :] = ranks_row.astype(jnp.int32)
    order_ref[...] = jnp.where(at == place, 1.0, 0.0).astype(BF16)
    room = ROOMS[0]
    wide = lax.broadcasted_iota(jnp.int32, pick_ref.shape, 1)
    block = wide // room
    distance = jnp.where(block < PLANES, block, block - PLANES)
    wanted = lax.bitwise_xor(distance, jnp.broadcast_to(me // 4, distance.shape)).astype(F32)
    found = (planes[:, :1] == wanted) & (ranks == (wide % room).astype(F32))
    pick_ref[...] = jnp.where(found, 1.0, 0.0).astype(BF16)
    most = jnp.max(ranks_row)
    rounds_ref[0] = (most >= room).astype(jnp.int32) + (most >= room + ROOMS[1]).astype(jnp.int32)


def low_rows(x_parts, down, table, distance):
    total = distance.shape[0]
    rank = down.shape[0]
    return pl.pallas_call(
        low_kernel,
        out_shape=[
            jax.ShapeDtypeStruct((total, rank), BF16),
            jax.ShapeDtypeStruct((2, total), jnp.int32),
            jax.ShapeDtypeStruct((total, (PLANES + len(ROWS)) * ROOMS[0]), BF16),
            jax.ShapeDtypeStruct((total, total), BF16),
            jax.ShapeDtypeStruct((1,), jnp.int32),
        ],
        in_specs=[VMEM] * 8,
        out_specs=[VMEM] * 4 + [pl.BlockSpec(memory_space=pltpu.SMEM)],
        compiler_params=pltpu.CompilerParams(vmem_limit_bytes=8 * 1024 * 1024),
        cost_estimate=pl.CostEstimate(flops=0, bytes_accessed=4096, transcendentals=0),
        name="low_rows",
    )(*x_parts, down, table, distance[None, :], distance[:, None])


def delta_kernel(plan, width, e_ref, *refs):
    parts, outs = refs[: len(refs) - len(plan)], refs[len(refs) - len(plan) :]
    e = e_ref[...]
    chip = 2 * parts[0].shape[0]
    if e.shape[1] > chip:
        parts = (*parts[:-2], jnp.concatenate([parts[-2][...], parts[-1][...]], axis=1))
        shape = (e.shape[1] - chip,) * 2
        half = jnp.broadcast_to(lax.axis_index("groups") * (chip // 4), shape)
        here, there = lax.broadcasted_iota(jnp.int32, shape, 0), lax.broadcasted_iota(jnp.int32, shape, 1)
        turn = jnp.where(lax.bitwise_xor(here, half) == there, 1.0, 0.0).astype(BF16)
        beyond = jnp.dot(e[:, chip:], turn, preferred_element_type=F32).astype(BF16)
        e = jnp.concatenate([e[:, :chip], beyond], axis=1)
    for pieces, out in zip(plan, outs):
        stacked = jnp.concatenate(
            [parts[n][at : at + rows, i * width : (i + 1) * width] for n, i, at, rows in pieces], axis=0
        )
        out[...] = jnp.dot(e[:, : stacked.shape[0]], stacked, preferred_element_type=F32).astype(BF16)


def delta_rows(e, parts, plan, width):
    rows = e.shape[0]
    n = len(plan)
    return pl.pallas_call(
        functools.partial(delta_kernel, plan, width),
        out_shape=[jax.ShapeDtypeStruct((rows, width), BF16)] * n,
        in_specs=[VMEM] * (1 + len(parts)),
        out_specs=[VMEM] * n,
        compiler_params=pltpu.CompilerParams(vmem_limit_bytes=8 * 1024 * 1024),
        cost_estimate=pl.CostEstimate(flops=0, bytes_accessed=4096, transcendentals=0),
        name="delta_rows",
    )(e, *parts)


BLOCK = 512
SLOTS = 3
AHEAD = 4


def fetch_kernel(first, after_ref, ref, head_ref, sem):
    copy = pltpu.make_async_copy(ref.at[pl.ds(first, head_ref.shape[0])], head_ref, sem)
    copy.start()
    copy.wait()


def fetch(after, matrix):
    shape = jax.ShapeDtypeStruct((AHEAD * BLOCK, matrix.shape[1]), BF16)
    return pl.pallas_call(
        functools.partial(fetch_kernel, 0),
        out_shape=shape,
        in_specs=[ANY, HBM],
        out_specs=VMEM,
        scratch_shapes=[pltpu.SemaphoreType.DMA],
        compiler_params=pltpu.CompilerParams(vmem_limit_bytes=4 * 1024 * 1024),
        cost_estimate=pl.CostEstimate(flops=0, bytes_accessed=8 * shape.size, transcendentals=0),
        name="fetch",
    )(after, matrix)


def base_kernel(steps, rows, *refs):
    x_refs, (g_ref, u_ref, g_head, u_head), refs = refs[:4], refs[4:8], refs[8:]
    gate_ref, up_ref, x_held, g_held, u_held, x_sems, g_sems, u_sems = refs

    def weights(k, slot):
        at = pl.ds(pl.multiple_of(k * BLOCK, BLOCK), BLOCK)
        return (
            pltpu.make_async_copy(g_ref.at[at], g_held.at[slot], g_sems.at[slot]),
            pltpu.make_async_copy(u_ref.at[at], u_held.at[slot], u_sems.at[slot]),
        )

    columns = pl.ds(0, steps * BLOCK)
    loads = [
        pltpu.make_async_copy(ref.at[:, columns], x_held.at[pl.ds(i * rows, rows)], x_sems.at[i])
        for i, ref in enumerate(x_refs)
    ]
    for copy in loads:
        copy.start()
    for k in range(SLOTS):
        for copy in weights(AHEAD + k, k):
            copy.start()
    for copy in loads:
        copy.wait()
    x = x_held[:, : AHEAD * BLOCK]
    gate_ref[...] = jnp.dot(x, g_head[...], preferred_element_type=F32)
    up_ref[...] = jnp.dot(x, u_head[...], preferred_element_type=F32)

    def step(n, carry):
        slot = lax.rem(n, SLOTS)
        k = n + AHEAD
        gate_copy, up_copy = weights(k, slot)
        x = x_held[:, pl.ds(pl.multiple_of(k * BLOCK, BLOCK), BLOCK)]
        gate_copy.wait()
        gate_ref[...] += jnp.dot(x, g_held[slot], preferred_element_type=F32)
        up_copy.wait()
        up_ref[...] += jnp.dot(x, u_held[slot], preferred_element_type=F32)

        @pl.when(k + SLOTS < steps)
        def _():
            for copy in weights(k + SLOTS, slot):
                copy.start()

        return carry

    lax.fori_loop(0, steps - AHEAD, step, 0)


def base(x_parts, gate_matrix, up_matrix, heads):
    depth, width = gate_matrix.shape
    steps = depth // BLOCK
    rows = x_parts[0].shape[0]
    total = rows * len(x_parts)
    shape = jax.ShapeDtypeStruct((total, width), F32)
    return pl.pallas_call(
        functools.partial(base_kernel, steps, rows),
        out_shape=[shape, shape],
        in_specs=[ANY] * len(x_parts) + [HBM] * 2 + [VMEM] * 2,
        out_specs=[VMEM, VMEM],
        scratch_shapes=[
            pltpu.VMEM((total, depth), BF16),
            pltpu.VMEM((SLOTS, BLOCK, width), BF16),
            pltpu.VMEM((SLOTS, BLOCK, width), BF16),
            pltpu.SemaphoreType.DMA((len(x_parts),)),
            pltpu.SemaphoreType.DMA((SLOTS,)),
            pltpu.SemaphoreType.DMA((SLOTS,)),
        ],
        compiler_params=pltpu.CompilerParams(vmem_limit_bytes=18 * 1024 * 1024),
        cost_estimate=pl.CostEstimate(
            flops=4 * total * depth * width, bytes_accessed=4 * depth * width, transcendentals=0
        ),
        name="base",
    )(*x_parts, gate_matrix, up_matrix, *heads)


def finish_kernel(step, gate_ref, up_ref, pick_ref, order_ref, *refs):
    rows_refs, (out_ref, held, sems) = refs[:-3], refs[-3:]
    writes = []
    for n in range(gate_ref.shape[1] // step):
        at = slice(n * step, (n + 1) * step)
        stacked = jnp.concatenate([ref[:, at] for ref in rows_refs], axis=0)
        gate = gate_ref[:, at] + jnp.dot(pick_ref[...], stacked, preferred_element_type=F32)
        hidden = (gate / (1.0 + jnp.exp(-gate)) * up_ref[:, at]).astype(BF16)
        held[:, at] = jnp.dot(order_ref[...], hidden, preferred_element_type=F32).astype(BF16)
        writes.append(pltpu.make_async_copy(held.at[:, at], out_ref.at[:, at], sems.at[n]))
        writes[-1].start()
    for copy in writes:
        copy.wait()


def finish(gate, up, pick, order, rows_by_plane):
    total, width = gate.shape
    n = 2 if width % (2 * LANES) == 0 else 1
    return pl.pallas_call(
        functools.partial(finish_kernel, width // n),
        out_shape=pltpu.HBM((total, width), BF16),
        in_specs=[VMEM] * (4 + len(rows_by_plane)),
        out_specs=HBM,
        scratch_shapes=[pltpu.VMEM((total, width), BF16), pltpu.SemaphoreType.DMA((n,))],
        compiler_params=pltpu.CompilerParams(vmem_limit_bytes=8 * 1024 * 1024),
        cost_estimate=pl.CostEstimate(flops=0, bytes_accessed=4 * total * width * 4, transcendentals=total * width),
        name="finish",
    )(gate, up, pick, order, *rows_by_plane)


def plane_shards(
    tokens,
    token_adapter_index,
    adapter_slot_index,
    gate_matrix,
    up_matrix,
    adapter_down_factor,
    adapter_up_factor,
):
    count = lax.axis_size("dp")
    me, y = lax.axis_index("dp"), lax.axis_index("groups")
    z = me // 4
    up_factor, gate_matrix, up_matrix = (
        pltpu.with_memory_space_constraint(v, pltpu.HBM) for v in (adapter_up_factor[0], gate_matrix, up_matrix)
    )
    own_rows, depth = tokens.shape
    total = own_rows * count
    width = gate_matrix.shape[1]
    rank = adapter_up_factor.shape[1]

    def swap(value, k):
        return lax.ppermute(value, "dp", [(d, d ^ k) for d in range(count)])

    def other(value):
        return lax.ppermute(value, "groups", [(0, 1), (1, 0)])

    index, cross, both = lax.optimization_barrier((token_adapter_index, *cut_cross(up_factor, width)))
    ids = jnp.broadcast_to(index.astype(BF16), (own_rows, LANES))
    packed = jnp.concatenate([tokens, ids], axis=1)
    cross, both = swap(cross, 2), swap(both, 3)
    second, third = swap(packed, 8), swap(packed, 12)
    pair = jnp.concatenate([packed, swap(packed, 2)], axis=0)
    remote = jnp.concatenate([second, third], axis=0)
    own_chip, own_plane, core_chip, core_plane = repack(up_factor, width)
    gate_head = fetch(own_plane, gate_matrix)
    close = jnp.concatenate([pair, swap(pair, 4)], axis=0)
    remote, down, core_chip, core_plane, gate_head, cross, both = lax.optimization_barrier(
        (remote, adapter_down_factor[0], core_chip, core_plane, gate_head, cross, both)
    )
    crossed = jnp.concatenate([cross, both], axis=0)
    part = width * 3 // 7 // LANES * LANES
    from_group = other(crossed[:, :part])
    remote = jnp.concatenate([remote, swap(remote, 2)], axis=0)
    core_chip, core_plane = swap(core_chip, 1), swap(core_plane, 1)
    heads = (gate_head, fetch(crossed, up_matrix))
    close, remote, heads, from_group = lax.optimization_barrier((close, remote, heads, from_group))
    x_parts = (close, remote, swap(close, 1), swap(remote, 1))
    distances = [0, 2, 4, 6, 8, 12, 10, 14]
    distances = distances + [k + 1 for k in distances]

    cross_parts = (crossed, from_group, other(crossed[:, part:]))
    half = rank // 2

    distance = jnp.array([k for k in distances for _ in range(own_rows)], jnp.int32)
    table = jnp.pad(adapter_slot_index, (0, LANES - count))[None, :]
    low, meta, first, order, rounds = low_rows(x_parts, down.T, table, distance)
    planes, ranks = meta[0], meta[1]

    chip_plan = tuple(((0, i, 0, rank), (1, i, 0, rank)) for i in range(2 * len(ROWS)))
    plane_plan = tuple(
        ((0, i, 0, rank), (1, i, 0, rank)) + tuple((n, i, at, half) for at in (0, half) for n in (2, 3))
        for i in range(len(FACTORS))
    )

    def chip_rows(e):
        return delta_rows(e, (own_chip, core_chip), chip_plan, width)

    def plane_rows(e):
        return delta_rows(e, (own_plane, core_plane, *cross_parts), plane_plan, width)

    def arrived(chip, plane):
        here, first, here_cross, first_cross = chip
        second, third = plane
        return [here, swap(first, 4), swap(second, 8), swap(third, 12), swap(here_cross, 2), first_cross]

    cross_low, both_low = swap(low, 2), swap(low, 3)
    chip = jnp.concatenate([low, swap(low, 1)], axis=1)
    by_chip = chip_rows(chip[: ROOMS[0]])
    by_chip, cross_low, both_low = lax.optimization_barrier((by_chip, cross_low, both_low))
    plane = jnp.concatenate([chip, cross_low, both_low], axis=1)
    by_plane = plane_rows(plane[: ROOMS[0]])
    first_cross = swap(by_chip[3], 6)
    by_plane, by_chip, x_parts = lax.optimization_barrier((by_plane, by_chip[:3], x_parts))
    by_chip = [*by_chip, first_cross]
    rows = arrived(by_chip, by_plane)
    gate, up = base(x_parts, gate_matrix, up_matrix, heads)

    def picked(start, room):
        at = jnp.where((ranks >= start) & (ranks < start + room), planes * room + ranks - start, -1)
        pick = (at[:, None] == jnp.arange(PLANES * room, dtype=jnp.int32)[None, :]).astype(BF16)
        return jnp.concatenate([pick, pick[:, : len(ROWS) * room]], axis=1)

    def short():
        return finish(gate, up, first, order, rows)

    def more(room):
        at = slice(ROOMS[0], ROOMS[0] + room)
        more_chip = chip_rows(chip[at])
        rest = arrived([*more_chip[:3], swap(more_chip[3], 6)], plane_rows(plane[at]))
        pick = jnp.concatenate([first, picked(ROOMS[0], room)], axis=1)
        return finish(gate, up, pick, order, rows + rest)

    return lax.switch(rounds[0], (short, lambda: more(ROOMS[1]), lambda: more(ROOMS[1] + ROOMS[2])))


def solution(mesh):
    in_specs = (
        P(("groups", "dp"), None),
        P(("groups", "dp"), None),
        P(),
        P(None, "dp"),
        P(None, "dp"),
        P("dp", None, None),
        P("dp", None, None),
    )
    out_specs = P("groups", "dp")
    shards = plane_shards if mesh.shape["dp"] == 16 and mesh.shape["groups"] == 2 else general_shards
    return jax.shard_map(shards, mesh=mesh, in_specs=in_specs, out_specs=out_specs, check_vma=False)
```
